256 devices in a mesh: dp: 32 (over z_hi, x, core), mp: 8 (over z_lo, y).
Axes of the slice: x: 4, y: 4, z: 8 (z_hi: 4, z_lo: 2; z = z_hi * 2 + z_lo), core: 2. Of those that a mesh axis runs over, the one named last changes fastest.
Arguments:
- grad: bfloat16 [4096, 4096], P('dp', 'mp')
- stat_state: float32 [64, 4096, 512], P('dp', 'mp'), as said below
- owners: int32 [8, 16], P('mp'), may hold values from 0 to 31, as said below
Outputs:
- update: bfloat16 [4096, 4096], P('dp', 'mp')
- new_state: float32 [64, 4096, 512], P('dp', 'mp')
The draws below stay inside these ranges and needn't reach their ends.
Inputs may be any that keep to these rules, and one draw needn't show every extreme that they name: `owners`: each row gives every factor of its column block an owner; no owner has more than 2 factors of a row and one has exactly 2. `stat_state`: every 512 x 512 block is symmetric positive definite.
All inputs are finite; a program needn't handle non-finite values.
Results may differ from the reference program's by a relative error of at most 0.013.
Values may be sent and summed in bfloat16 or wider, within the bound.
A program may use at most 128 MiB of HBM per device.

```python
import math
import jax
import jax.numpy as jnp
from jax import lax

D = 4096
BLOCK = 512
ITERS = 6
SLOTS = 2
OWNERS = 32
FACTORS = 16
N_MP = 8


def draw_grad(key, part):
    key = jax.random.fold_in(key, 3)
    first_key, second_key, third_key = jax.random.split(key, 3)
    width = BLOCK * N_MP
    shape = (D, width)
    base = jax.random.normal(first_key, shape, jnp.float32)
    row_scale = jnp.exp(jax.random.uniform(second_key, (D, 1), jnp.float32, 0.0, math.log(10.0)))
    col_scale = jnp.exp(jax.random.uniform(third_key, (1, width), jnp.float32, 0.0, math.log(10.0)))
    row_place = lax.broadcasted_iota(jnp.float32, shape, 0) / D
    col_place = lax.broadcasted_iota(jnp.float32, shape, 1) / width
    ramp = jnp.exp(math.log(3.0) * (row_place + col_place))
    return (0.1 * base * row_scale * col_scale * ramp).astype(jnp.bfloat16)


def draw_stat_state(key, part):
    key = jax.random.fold_in(key, 5)
    first_key, second_key = jax.random.split(key)
    total_blocks = OWNERS * SLOTS * N_MP
    top = math.log(100.0)
    spread = jnp.exp(jax.random.uniform(second_key, (total_blocks, BLOCK), jnp.float32, 0.0, top))
    rows = lax.broadcasted_iota(jnp.int32, (BLOCK, BLOCK), 0)
    cols = lax.broadcasted_iota(jnp.int32, (BLOCK, BLOCK), 1)
    eye = (rows == cols).astype(jnp.float32)

    def one_block(index):
        block_key = jax.random.fold_in(first_key, index)
        factor = jax.random.normal(block_key, (BLOCK, BLOCK), jnp.float32)
        product = jnp.dot(factor, factor.T, precision=lax.Precision.HIGHEST) / BLOCK
        product = 0.5 * (product + product.T)
        row_spread = lax.dynamic_index_in_dim(spread, index, 0, keepdims=False)
        root_spread = jnp.sqrt(row_spread)
        scaled = product * root_spread[:, None] * root_spread[None, :]
        return BLOCK * (scaled + eye * row_spread[:, None])
    matrix = lax.map(one_block, jnp.arange(total_blocks, dtype=jnp.int32))
    return matrix.reshape(OWNERS * SLOTS, N_MP * BLOCK, BLOCK)


def draw_owners(key, part):
    key = jax.random.fold_in(key, 11)

    def one_row(row_key):
        rank_key, order_key = jax.random.split(row_key)
        ranks = jax.random.permutation(rank_key, FACTORS)
        order = jax.random.permutation(order_key, OWNERS)
        pick = jnp.where(ranks < SLOTS, 0, 1 + (ranks - SLOTS) % (OWNERS - 1))
        return order[pick].astype(jnp.int32)
    return jax.vmap(one_row)(jax.random.split(key, N_MP))


def setup_inputs(seed: int = 0) -> dict:
    seeds = jax.random.split(jax.random.key(seed), 4)
    return {
        "grad": draw_grad(jax.random.fold_in(seeds[3], 71), 0),
        "stat_state": draw_stat_state(jax.random.fold_in(seeds[3], 71), 0),
        "owners": draw_owners(jax.random.fold_in(seeds[3], 71), 0),
    }


BETA = 0.9
EPS = 1e-06

def newton_root(stat):
    order = stat.shape[0]
    scale = jnp.sqrt(jnp.sum(stat * stat) + EPS)
    iterate = jnp.eye(order, dtype=jnp.float32) * scale ** (-0.25)
    reduced = stat / scale
    for sweep_index in range(ITERS):
        reduced_low = reduced.astype(jnp.bfloat16)
        quarter = (reduced_low.astype(jnp.float32) * 0.25).astype(jnp.bfloat16)
        square_delta = (jnp.dot(quarter, quarter, preferred_element_type=jnp.float32) - 2.5 * quarter.astype(jnp.float32)).astype(jnp.bfloat16)
        fourth_delta = (jnp.dot(square_delta, square_delta, preferred_element_type=jnp.float32) + 3.125 * square_delta.astype(jnp.float32)).astype(jnp.bfloat16)
        iterate = 1.25 * iterate - jnp.dot(iterate.astype(jnp.bfloat16), quarter, preferred_element_type=jnp.float32)
        reduced = 2.44140625 * reduced + jnp.dot(fourth_delta, reduced_low, preferred_element_type=jnp.float32)
    return iterate

def slot_numbers(table):
    count = table.shape[0]
    later = lax.broadcasted_iota(jnp.int32, (count, count), 0)
    early = lax.broadcasted_iota(jnp.int32, (count, count), 1)
    same = table[:, None] == table[None, :]
    return lax.optimization_barrier(jnp.sum((same & (early < later)).astype(jnp.int32), axis=1)).astype(jnp.int32)

def reference(grad, stat_state, owners):
    nblocks = D // BLOCK
    count = 2 * nblocks
    high = lax.Precision.HIGHEST
    updates = []
    states = []
    for column in range(N_MP):
        part_grad = grad[:, column * BLOCK:(column + 1) * BLOCK]
        blocks = part_grad.reshape(nblocks, BLOCK, BLOCK).astype(jnp.float32)
        left = jnp.einsum('ijk,ilk->ijl', blocks, blocks, precision=high)
        right = jnp.einsum('ikj,ikl->ijl', blocks, blocks, precision=high)
        stats = jnp.stack([left, right], axis=1).reshape(count, BLOCK, BLOCK)
        table = owners[column]
        position = (table * SLOTS + slot_numbers(table)).astype(jnp.int32)
        state_part = stat_state[:, column * BLOCK:(column + 1) * BLOCK, :]
        mixed = BETA * state_part[position] + (1.0 - BETA) * stats
        states.append(state_part.at[position].set(mixed))
        roots = lax.map(newton_root, mixed).astype(jnp.bfloat16)
        left_roots = roots[0::2].astype(jnp.float32)
        right_roots = roots[1::2].astype(jnp.float32)
        first = jnp.einsum('ijk,ikl->ijl', left_roots, blocks, precision=high).astype(jnp.bfloat16)
        raw = jnp.einsum('ijk,ikl->ijl', first.astype(jnp.float32), right_roots, precision=high)
        updates.append(raw.reshape(D, BLOCK))
    raw_all = jnp.concatenate(updates, axis=1)
    grad_wide = grad.astype(jnp.float32)
    ratio = jnp.sqrt(jnp.sum(grad_wide * grad_wide) / (jnp.sum(raw_all * raw_all) + EPS))
    update = (raw_all * ratio).astype(jnp.bfloat16)
    new_state = jnp.concatenate(states, axis=1)
    return (update, new_state)
```

```python
import jax
import jax.numpy as jnp
from jax import lax
from jax.experimental import pallas as pl
from jax.experimental.pallas import tpu as pltpu
from jax.sharding import PartitionSpec as P

ITERS = 6
BETA = 0.9
EPS = 1e-06
MESH = pl.DeviceIdType.MESH
BF = jnp.bfloat16
F32 = jnp.float32

WIDTH = 512
TILE = 128
COUNT = 16
ROWS = 8
PARTS = 2
PAIRS = [(i, j) for i in range(4) for j in range(i, 4)]
PER = len(PAIRS) // PARTS


def block(ref, i, j):
    return ref[i * TILE:(i + 1) * TILE, j * TILE:(j + 1) * TILE]


def kernel(
    owners_hbm, grad, state_hbm, update, new_hbm,
    state, owners, positions, inverse,
    pack0, pack1, spread0, spread1, cross0, cross1, relay0, relay1, landed0, landed1,
    chosen0, chosen1, factor0, factor1, stat_pack0, stat_pack1, stat_all0, stat_all1,
    gfull, stat, stat_pick, stat_back,
    m_ref, x_ref, b_ref, p_ref, f_ref, roots, raw_ref, sums_a, sums_b,
    s1s, s1r, s2s, s2r, s3s, s3r, gs, gr, r1s, r1r, r2s, r2r, r3s, r3r, rts, rtr, pas, par, pbs, pbr, loc,
):
    packs, spreads, crosses = (pack0, pack1), (spread0, spread1), (cross0, cross1)
    relays, landeds, chosens, factors = (relay0, relay1), (landed0, landed1), (chosen0, chosen1), (factor0, factor1)
    stat_packs, stat_alls = (stat_pack0, stat_pack1), (stat_all0, stat_all1)
    me = lax.axis_index("dp")
    mp = lax.axis_index("mp")
    row, r = lax.div(me, 8), lax.rem(me, 8)
    x, c = lax.div(r, 2), lax.rem(r, 2)
    zlo, y = lax.div(mp, 4), lax.rem(mp, 4)
    quad = lax.rem(x, 2) * 2 + c

    def send(src, dst, ssem, rsem, dp, mp_to=None):
        copy = pltpu.make_async_remote_copy(
            src_ref=src, dst_ref=dst, send_sem=ssem, recv_sem=rsem,
            device_id=(dp, mp if mp_to is None else mp_to), device_id_type=MESH,
        )
        copy.start()
        return copy

    def row_peer(t):
        return lax.rem(r + t, 8)

    def plane_peer(dx, dy):
        to_x, to_y = lax.rem(x + dx, 4), lax.rem(y + dy, 4)
        return row * 8 + to_x * 2 + c, zlo * 4 + to_y

    def column_peer(dh, dl, dc):
        to_row, to_lo, to_c = lax.rem(row + dh, 4), lax.rem(zlo + dl, 2), lax.rem(c + dc, 2)
        return to_row * 8 + x * 2 + to_c, to_lo * 4 + y

    plane = [(dx, dy) for dx in range(4) for dy in range(4) if dx or dy]
    column = [(dh, dl, dc) for dh in range(4) for dl in range(2) for dc in range(2) if dh or dl or dc]

    loads = [pltpu.make_async_copy(state_hbm.at[k], state.at[k], loc.at[k]) for k in range(2)]
    for load in loads:
        load.start()
    own_grad = pltpu.make_async_copy(grad, gfull.at[quad], loc.at[2])
    own_grad.start()
    own_table = pltpu.make_async_copy(owners_hbm, owners, loc.at[3])
    own_table.start()
    barrier = pltpu.get_barrier_semaphore()
    greeted = [(row * 8 + row_peer(t), mp) for t in range(1, ROWS)]
    greeted += [plane_peer(dx, dy) for dx, dy in plane if dy]
    greeted += [column_peer(*d) for d in column if d[0] or d[1]]
    for peer in greeted:
        pl.semaphore_signal(barrier, inc=1, device_id=peer, device_id_type=MESH)

    for k in range(2):
        loads[k].wait()
        for n, (i, j) in enumerate(PAIRS):
            piece = block(state.at[k], i, j).astype(BF).reshape(ROWS, 16, TILE)
            packs[n // PER][:, k, n % PER] = piece
    for part in range(PARTS):
        spreads[part][pl.ds(2 * r, 2)] = packs[part][r]
    pl.semaphore_wait(barrier, len(greeted))

    stage1 = []
    for part in range(PARTS):
        copies = []
        for t in range(1, ROWS):
            peer = row_peer(t)
            s = part * 7 + t - 1
            copies.append(send(packs[part].at[peer], spreads[part].at[pl.ds(2 * r, 2)], s1s.at[s], s1r.at[s], row * 8 + peer))
        stage1.append(copies)
    own_grad.wait()
    other = x + 1 - 2 * lax.rem(x, 2)
    sibling = row * 8 + x * 2 + 1 - c
    own_rows = gfull.at[quad]
    g_copies = [
        send(own_rows, own_rows, gs.at[0], gr.at[0], row * 8 + other * 2 + c),
        send(own_rows, own_rows, gs.at[1], gr.at[1], sibling),
    ]

    own_table.wait()
    table = [owners[0, f] for f in range(COUNT)]
    place = []
    for f in range(COUNT):
        slot = jnp.int32(0)
        for g in range(f):
            slot = slot + jnp.where(table[g] == table[f], 1, 0)
        place.append(table[f] * 2 + slot)
        positions[f] = place[f]

    def invert(index, carry):
        target = row * 16 + index
        found = jnp.int32(-1)
        for f in range(COUNT):
            found = jnp.where(positions[f] == target, f, found)
        inverse[index] = found
        return carry

    lax.fori_loop(0, COUNT, invert, 0)

    wide = gfull[quad].astype(F32)
    grad_sum = jnp.sum(wide * wide, axis=0, keepdims=True)
    grad_sum = grad_sum[:, :128] + grad_sum[:, 128:256] + grad_sum[:, 256:384] + grad_sum[:, 384:]

    def turned(by):
        return lax.rem(row + by, 4)

    ways = (1, 3)
    stage2 = []
    for part, way in enumerate(ways):
        for copy in stage1[part]:
            copy.wait_recv()

        def own(to_row, q):
            return spreads[part][jnp.clip(positions[to_row * 4 + q] - row * 16, 0, 15)]

        s = part * 3
        copies = []
        for q in range(4):
            crosses[part][0, q] = own(turned(2), q)
        copies.append(send(crosses[part].at[0], relays[part], s2s.at[s], s2r.at[s], turned(way) * 8 + r))
        for q in range(4):
            crosses[part][1, q] = own(turned(4 - way), q)
        copies.append(send(crosses[part].at[1], landeds[part].at[pl.ds(8, 4)], s2s.at[s + 1], s2r.at[s + 1], turned(4 - way) * 8 + r))
        for q in range(4):
            landeds[part][q] = own(row, q)
        stage2.append(copies)
    for part, way in enumerate(ways):
        stage2[part][0].wait_recv()
        s = part * 3
        for q in range(4):
            place_q = positions[turned(way) * 4 + q] - row * 16
            is_own = (place_q >= 0) & (place_q < 16)
            crosses[part][2, q] = jnp.where(is_own, spreads[part][jnp.clip(place_q, 0, 15)], relays[part][q])
        stage2[part].append(send(crosses[part].at[2], landeds[part].at[pl.ds(4, 4)], s2s.at[s + 2], s2r.at[s + 2], turned(way) * 8 + r))

    g_copies[0].wait_recv()
    other_rows = gfull.at[lax.rem(other, 2) * 2 + c]
    g_copies.append(send(other_rows, other_rows, gs.at[2], gr.at[2], sibling))
    g_copies[1].wait_recv()
    g_copies[2].wait_recv()
    g = gfull[...].reshape(WIDTH, WIDTH)

    @pl.when(c == 0)
    def _():
        stat[...] = lax.dot_general(g, g, (((1,), (1,)), ((), ())), preferred_element_type=F32)

    @pl.when(c == 1)
    def _():
        stat[...] = lax.dot_general(g.T, g, (((1,), (0,)), ((), ())), preferred_element_type=F32)

    mine = row * 4 + lax.div(x, 2) * 2 + c
    outer = lax.rem(x + 3 + 2 * lax.rem(x, 2), 4)
    back1 = []
    for part in range(PARTS):
        for n, (i, j) in enumerate(PAIRS):
            if n // PER == part:
                stat_packs[part][:, n % PER] = block(stat, i, j).astype(BF).reshape(ROWS, 16, TILE)
        stat_alls[part][mine] = stat_packs[part][r]
        copies = []
        for s, (to_x, to_c) in enumerate([(x, 1 - c), (outer, c), (outer, 1 - c)]):
            to, s = to_x * 2 + to_c, s + part * 3
            copies.append(send(stat_packs[part].at[to], stat_alls[part].at[mine], r1s.at[s], r1r.at[s], row * 8 + to))
        back1.append(copies)

    stage3 = []
    back2 = []
    for part in range(PARTS):
        stage2[part][1].wait_recv()
        stage2[part][2].wait_recv()
        for q in range(4):
            origin = lax.div(positions[row * 4 + q], 16)
            t = lax.rem(row - origin + 4, 4) if ways[part] == 1 else lax.rem(origin - row + 4, 4)
            chosens[part][q] = landeds[part][jnp.where(t >= 2, t - 1, t) * 4 + q]
        copies = []
        for t in range(1, ROWS):
            peer = row_peer(t)
            q = lax.div(peer, 4) * 2 + lax.rem(peer, 2)
            s = part * 7 + t - 1
            copies.append(send(chosens[part].at[q], factors[part].at[r], s3s.at[s], s3r.at[s], row * 8 + peer))
        factors[part][r] = chosens[part][lax.div(x, 2) * 2 + c]
        stage3.append(copies)

        if part == 0:
            for back, way in enumerate(ways):
                for copy in back1[back]:
                    copy.wait_recv()
                here = stat_alls[back].at[pl.ds(4 * row, 4)]
                s = back * 3
                copies = []
                for t, by in enumerate((way, 4 - way)):
                    copies.append(send(here, here, r2s.at[s + t], r2r.at[s + t], turned(by) * 8 + r))
                back2.append(copies)

    norm = jnp.zeros((TILE, TILE), F32)
    for n, (i, j) in enumerate(PAIRS):
        if n % PER == 0:
            for copy in stage3[n // PER]:
                copy.wait_recv()
        old = factors[n // PER][:, n % PER].reshape(TILE, TILE).astype(F32)
        mixed = BETA * old + (1.0 - BETA) * block(stat, i, j)
        m_ref[i * TILE:(i + 1) * TILE, j * TILE:(j + 1) * TILE] = mixed
        if i == j:
            norm = norm + mixed * mixed
        else:
            m_ref[j * TILE:(j + 1) * TILE, i * TILE:(i + 1) * TILE] = mixed.T
            norm = norm + 2.0 * (mixed * mixed)
    total = jnp.sum(jnp.sum(norm, axis=0, keepdims=True), axis=1, keepdims=True)
    scale = jnp.sqrt(total + EPS)
    inverse_scale = 1.0 / scale
    start = lax.rsqrt(jnp.sqrt(scale))
    start_low = start.astype(BF).astype(F32)

    HALF = WIDTH // 2
    for h in range(2):
        rows = pl.ds(h * HALF, HALF)
        reduced = m_ref[rows] * inverse_scale
        m_ref[rows] = reduced
        low = reduced.astype(BF)
        b_ref[rows] = low
        at = lax.broadcasted_iota(jnp.int32, (HALF, WIDTH), 0) + h * HALF
        eye = at == lax.broadcasted_iota(jnp.int32, (HALF, WIDTH), 1)
        x_ref[rows] = jnp.where(eye, 1.25 * start, 0.0) - (0.25 * start_low) * low.astype(F32)

    def dot(a, b):
        return jnp.dot(a, b, preferred_element_type=F32)

    halves = [pl.ds(h * HALF, HALF) for h in range(2)]

    def advance():
        for cols in halves:
            p_ref[:, cols] = (dot(b_ref[...], b_ref[:, cols]) * 0.0625 - 0.625 * b_ref[:, cols].astype(F32)).astype(BF)
        for cols in halves:
            f_ref[:, cols] = (dot(p_ref[...], p_ref[:, cols]) + 3.125 * p_ref[:, cols].astype(F32)).astype(BF)
        for cols in halves:
            m_ref[:, cols] = 2.44140625 * m_ref[:, cols] + dot(f_ref[...], b_ref[:, cols])

    def step(index, carry):
        b_ref[...] = m_ref[...].astype(BF)
        low = x_ref[...].astype(BF)
        for cols in halves:
            x_ref[:, cols] = 1.25 * x_ref[:, cols] - 0.25 * dot(low, b_ref[:, cols])
        advance()
        return carry

    advance()

    for part, way in enumerate(ways):
        back2[part][0].wait_recv()
        here = stat_alls[part].at[pl.ds(4 * turned(4 - way), 4)]
        s = part * 3 + 2
        back2[part].append(send(here, here, r2s.at[s], r2r.at[s], turned(way) * 8 + r))
    lax.fori_loop(1, 4, step, 0)

    for copies in back2:
        copies[1].wait_recv()
        copies[2].wait_recv()
    back3 = []
    for t in range(1, ROWS):
        peer = row_peer(t)
        for k in range(2):
            for part in range(PARTS):
                stat_pick[t - 1, k, part] = stat_alls[part][jnp.maximum(inverse[2 * peer + k], 0)]
        back3.append(send(stat_pick.at[t - 1], stat_back.at[r], r3s.at[t - 1], r3r.at[t - 1], row * 8 + peer))
    for k in range(2):
        for part in range(PARTS):
            stat_back[r, k, part] = stat_alls[part][jnp.maximum(inverse[2 * r + k], 0)]

    lax.fori_loop(4, ITERS - 1, step, 0)
    for h in range(2):
        rows = pl.ds(h * HALF, HALF)
        b_ref[rows] = m_ref[rows].astype(BF)
    root_copies = []
    for h in range(4):
        rows = pl.ds(h * TILE, TILE)
        last = 1.25 * x_ref[rows] - 0.25 * dot(x_ref[rows].astype(BF), b_ref[...])
        roots[c, rows] = last.astype(BF)
        here = roots.at[c, rows]
        root_copies.append(send(here, here, rts.at[h], rtr.at[h], sibling))

    for copy in root_copies:
        copy.wait_recv()
    left = roots[0, pl.ds(quad * TILE, TILE)]
    first = dot(left, gfull[...].reshape(WIDTH, WIDTH)).astype(BF)
    raw = dot(first, roots[1])
    raw_ref[...] = raw
    raw_sum = jnp.sum(raw * raw, axis=0, keepdims=True)
    raw_sum = raw_sum[:, :128] + raw_sum[:, 128:256] + raw_sum[:, 256:384] + raw_sum[:, 384:]

    v = row * 4 + zlo * 2 + c
    sums_a[v, :, :128] = grad_sum
    sums_a[v, :, 128:] = raw_sum
    round_a = []
    for s, d in enumerate(column):
        dp, to_mp = column_peer(*d)
        round_a.append(send(sums_a.at[v], sums_a.at[v], pas.at[s], par.at[s], dp, to_mp))
    for copy in round_a:
        copy.wait_recv()
    u = x * 4 + y
    sums_b[u] = jnp.sum(sums_a[...], axis=0)
    round_b = []
    for s, d in enumerate(plane):
        dp, to_mp = plane_peer(*d)
        round_b.append(send(sums_b.at[u], sums_b.at[u], pbs.at[s], pbr.at[s], dp, to_mp))

    for copy in back3:
        copy.wait_recv()
    stores = []
    for k in range(2):
        present = inverse[2 * r + k] >= 0
        for n, (i, j) in enumerate(PAIRS):
            got = stat_back[:, k, n // PER, n % PER].reshape(TILE, TILE).astype(F32)
            for a, b, value in ((i, j, got),) + (((j, i, got.T),) if i != j else ()):
                old = state[k, a * TILE:(a + 1) * TILE, b * TILE:(b + 1) * TILE]
                state[k, a * TILE:(a + 1) * TILE, b * TILE:(b + 1) * TILE] = jnp.where(
                    present, BETA * old + (1.0 - BETA) * value, old
                )
        store = pltpu.make_async_copy(state.at[k], new_hbm.at[k], loc.at[k])
        store.start()
        stores.append(store)

    for copy in round_b:
        copy.wait_recv()
    both = jnp.sum(sums_b[...], axis=0)
    grad_total = jnp.sum(both[:, :128], axis=1, keepdims=True)
    raw_total = jnp.sum(both[:, 128:], axis=1, keepdims=True)
    ratio = jnp.sqrt(grad_total / (raw_total + EPS))
    update[...] = (raw_ref[...] * ratio).astype(BF)

    for copies in stage1 + stage2 + stage3 + back1 + back2 + [g_copies, back3, root_copies, round_a, round_b]:
        for copy in copies:
            copy.wait_send()
    for store in stores:
        store.wait()


def shards(grad, stat_state, owners):
    dma = pltpu.SemaphoreType.DMA
    vm = pltpu.VMEM

    def two(*shape):
        return [vm(shape + (PER, 16, TILE), BF) for _ in range(PARTS)]

    sems = []
    for count in (7 * PARTS, 3 * PARTS, 7 * PARTS, 3, 3 * PARTS, 3 * PARTS, 7, 4, 15, 15):
        sems += [dma((count,)), dma((count,))]
    square = (WIDTH, WIDTH)
    results = pl.pallas_call(
        kernel,
        out_shape=(
            jax.ShapeDtypeStruct((TILE, WIDTH), BF),
            jax.ShapeDtypeStruct((2, WIDTH, WIDTH), F32),
        ),
        in_specs=[
            pl.BlockSpec(memory_space=pltpu.HBM),
            pl.BlockSpec(memory_space=pltpu.HBM),
            pl.BlockSpec(memory_space=pltpu.HBM),
        ],
        out_specs=(pl.BlockSpec(memory_space=pltpu.VMEM), pl.BlockSpec(memory_space=pl.ANY)),
        scratch_shapes=[
            vm((2, WIDTH, WIDTH), F32),
            pltpu.SMEM((1, COUNT), jnp.int32),
            pltpu.SMEM((COUNT,), jnp.int32),
            pltpu.SMEM((COUNT,), jnp.int32),
            *two(ROWS, 2), *two(16), *two(3, 4), *two(4), *two(12), *two(4), *two(ROWS), *two(ROWS), *two(COUNT),
            vm((4, TILE, WIDTH), BF),
            vm(square, F32),
            vm((7, 2, PARTS, PER, 16, TILE), BF),
            vm((ROWS, 2, PARTS, PER, 16, TILE), BF),
            vm(square, F32), vm(square, F32), vm(square, BF), vm(square, BF), vm(square, BF),
            vm((2, WIDTH, WIDTH), BF),
            vm((TILE, WIDTH), F32),
            vm((16, 1, 256), F32),
            vm((16, 1, 256), F32),
            *sems,
            dma((4,)),
        ],
        compiler_params=pltpu.CompilerParams(
            collective_id=0, has_side_effects=True, vmem_limit_bytes=60 * 1024 * 1024
        ),
    )(owners, grad, stat_state)
    hbm = pl.BlockSpec(memory_space=pltpu.HBM)
    return pl.pallas_call(
        hand_over,
        out_shape=tuple(jax.ShapeDtypeStruct(a.shape, a.dtype) for a in results),
        in_specs=[hbm, hbm],
        out_specs=(hbm, hbm),
        scratch_shapes=[vm((2, WIDTH, WIDTH), F32), vm((TILE, WIDTH), BF), dma((2, 9))],
        compiler_params=pltpu.CompilerParams(vmem_limit_bytes=60 * 1024 * 1024),
    )(*results)


def hand_over(update, new, update_out, new_out, held, held_update, sems):
    ways = [(update, held_update, update_out)]
    for s in range(8):
        rows = pl.ds(s % 4 * TILE, TILE)
        ways.append((new.at[s // 4, rows], held.at[s // 4, rows], new_out.at[s // 4, rows]))
    into = [pltpu.make_async_copy(a, b, sems.at[0, s]) for s, (a, b, _) in enumerate(ways)]
    out = [pltpu.make_async_copy(b, c, sems.at[1, s]) for s, (_, b, c) in enumerate(ways)]
    for copy in into:
        copy.start()
    for copy, then in zip(into, out):
        copy.wait()
        then.start()
    for copy in out:
        copy.wait()


def solution(mesh):
    return jax.shard_map(
        shards,
        mesh=mesh,
        in_specs=(P("dp", "mp"), P("dp", "mp", None), P("mp", None)),
        out_specs=(P("dp", "mp"), P("dp", "mp", None)),
        check_vma=False,
    )
```

```python
import jax
import jax.numpy as jnp
from jax import lax
from jax.experimental import pallas as pl
from jax.experimental.pallas import tpu as pltpu
from jax.sharding import PartitionSpec as P

ITERS = 6
BETA = 0.9
EPS = 1e-06
MESH = pl.DeviceIdType.MESH
BF = jnp.bfloat16
F32 = jnp.float32

WIDTH = 512
TILE = 128
COUNT = 16
ROWS = 8
PAIRS = [(i, j) for i in range(4) for j in range(i + 1, 4)]
SIZES = (3, 2, 2, 2)
PARTS = len(SIZES)
SPOT = [(p, n) for p, size in enumerate(SIZES) for n in range(size)]
BACK_SIZES = (5, 4)
BACKS = len(BACK_SIZES)
BACK_SPOT = [(p, n) for p, size in enumerate(BACK_SIZES) for n in range(size)]


def block(ref, i, j):
    return ref[i * TILE:(i + 1) * TILE, j * TILE:(j + 1) * TILE]


def packed(ref):
    half = TILE // 2
    diag = [block(ref, d, d) for d in range(4)]
    upper = [jnp.concatenate([diag[d][:half], diag[d + 1][:half]], axis=0) for d in (0, 2)]
    left = lax.broadcasted_iota(jnp.int32, (half, TILE), 1) < half
    lower = [jnp.where(left, pltpu.roll(diag[d + 1][half:], half, 1), diag[d][half:]) for d in (0, 2)]
    blocks = upper + [jnp.concatenate(lower, axis=0)] + [block(ref, i, j) for i, j in PAIRS]
    return [b.astype(BF).reshape(ROWS, 16, TILE) for b in blocks]


def unpacked(get):
    half = TILE // 2
    low = lax.broadcasted_iota(jnp.int32, (TILE, TILE), 0) >= half
    left = lax.broadcasted_iota(jnp.int32, (TILE, TILE), 1) < half
    corners = get(2)
    for d in range(4):
        upper = get(d // 2)[d % 2 * half:(d % 2 + 1) * half]
        corner = corners[d // 2 * half:(d // 2 + 1) * half]
        if d % 2:
            corner = pltpu.roll(corner, half, 1)
        whole = jnp.concatenate([upper, corner], axis=0)
        yield d, d, jnp.where(low & left, whole.T, whole)
    for n, (i, j) in enumerate(PAIRS):
        yield i, j, get(3 + n)


def kernel(
    owners_hbm, grad, state_hbm, update, new_hbm,
    state, owners, positions, inverse,
    packs, spreads, crosses, relays, landeds, chosens, factors, stat_packs, stat_alls,
    stat_picks, stat_backs, gfull, stat,
    m_ref, x_ref, b_ref, p_ref, f_ref, xl_ref, roots, raw_ref, sums_a, sums_b,
    s1s, s1r, s2s, s2r, s3s, s3r, gs, gr, r1s, r1r, r2s, r2r, r3s, r3r, rts, rtr, pas, par, pbs, pbr, loc,
):
    me = lax.axis_index("dp")
    mp = lax.axis_index("mp")
    row, r = lax.div(me, 8), lax.rem(me, 8)
    x, c = lax.div(r, 2), lax.rem(r, 2)
    zlo, y = lax.div(mp, 4), lax.rem(mp, 4)
    quad = lax.rem(x, 2) * 2 + c

    def send(src, dst, ssem, rsem, dp, mp_to=None):
        copy = pltpu.make_async_remote_copy(
            src_ref=src, dst_ref=dst, send_sem=ssem, recv_sem=rsem,
            device_id=(dp, mp if mp_to is None else mp_to), device_id_type=MESH,
        )
        copy.start()
        return copy

    def sent(groups):
        for copies in groups:
            for copy in copies:
                copy.wait_send()

    def row_peer(t):
        return lax.rem(r + t, 8)

    def plane_peer(dx, dy):
        to_x, to_y = lax.rem(x + dx, 4), lax.rem(y + dy, 4)
        return row * 8 + to_x * 2 + c, zlo * 4 + to_y

    def column_peer(dh, dl, dc):
        to_row, to_lo, to_c = lax.rem(row + dh, 4), lax.rem(zlo + dl, 2), lax.rem(c + dc, 2)
        return to_row * 8 + x * 2 + to_c, to_lo * 4 + y

    plane = [(dx, dy) for dx in range(4) for dy in range(4) if dx or dy]
    column = [(dh, dl, dc) for dh in range(4) for dl in range(2) for dc in range(2) if dh or dl or dc]

    loads = [pltpu.make_async_copy(state_hbm.at[k], state.at[k], loc.at[k]) for k in range(2)]
    for load in loads:
        load.start()
    own_grad = pltpu.make_async_copy(grad, gfull.at[quad], loc.at[2])
    own_grad.start()
    own_table = pltpu.make_async_copy(owners_hbm, owners, loc.at[3])
    own_table.start()
    barrier = pltpu.get_barrier_semaphore()
    greeted = [(row * 8 + row_peer(t), mp) for t in range(1, ROWS)]
    greeted += [plane_peer(dx, dy) for dx, dy in plane if dy]
    greeted += [column_peer(*d) for d in column if d[0] or d[1]]
    for peer in greeted:
        pl.semaphore_signal(barrier, inc=1, device_id=peer, device_id_type=MESH)

    for k in range(2):
        loads[k].wait()
        for (part, at), piece in zip(SPOT, packed(state.at[k])):
            packs[part][:, k, at] = piece
    for part in range(PARTS):
        spreads[part][pl.ds(2 * r, 2)] = packs[part][r]
    pl.semaphore_wait(barrier, len(greeted))

    stage1 = []
    for part in range(PARTS):
        copies = []
        for t in range(1, ROWS):
            peer = row_peer(t)
            s = part * 7 + t - 1
            copies.append(send(packs[part].at[peer], spreads[part].at[pl.ds(2 * r, 2)], s1s.at[s], s1r.at[s], row * 8 + peer))
        stage1.append(copies)
    own_grad.wait()
    other = x + 1 - 2 * lax.rem(x, 2)
    sibling = row * 8 + x * 2 + 1 - c
    own_rows = gfull.at[quad]
    g_copies = [
        send(own_rows, own_rows, gs.at[0], gr.at[0], row * 8 + other * 2 + c),
        send(own_rows, own_rows, gs.at[1], gr.at[1], sibling),
    ]

    own_table.wait()
    table = [owners[0, f] for f in range(COUNT)]
    place = []
    for f in range(COUNT):
        slot = jnp.int32(0)
        for g in range(f):
            slot = slot + jnp.where(table[g] == table[f], 1, 0)
        place.append(table[f] * 2 + slot)
        positions[f] = place[f]

    def invert(index, carry):
        target = row * 16 + index
        found = jnp.int32(-1)
        for f in range(COUNT):
            found = jnp.where(positions[f] == target, f, found)
        inverse[index] = found
        return carry

    lax.fori_loop(0, COUNT, invert, 0)

    wide = gfull[quad].astype(F32)
    grad_sum = jnp.sum(wide * wide, axis=0, keepdims=True)
    grad_sum = grad_sum[:, :128] + grad_sum[:, 128:256] + grad_sum[:, 256:384] + grad_sum[:, 384:]

    def turned(by):
        return lax.rem(row + by, 4)

    ways = (1, 3) * (PARTS // 2)
    back_ways = (1, 3)
    stage2 = []

    def cross(part):
        way = ways[part]
        for copy in stage1[part]:
            copy.wait_recv()

        def own(to_row, q):
            return spreads[part][jnp.clip(positions[to_row * 4 + q] - row * 16, 0, 15)]

        s = part * 3
        copies = []
        for q in range(4):
            crosses[part][0, q] = own(turned(2), q)
        copies.append(send(crosses[part].at[0], relays[part], s2s.at[s], s2r.at[s], turned(way) * 8 + r))
        for q in range(4):
            crosses[part][1, q] = own(turned(4 - way), q)
        copies.append(send(crosses[part].at[1], landeds[part].at[pl.ds(8, 4)], s2s.at[s + 1], s2r.at[s + 1], turned(4 - way) * 8 + r))
        for q in range(4):
            landeds[part][q] = own(row, q)
        stage2.append(copies)

    def merge(part):
        way = ways[part]
        stage2[part][0].wait_recv()
        s = part * 3
        for q in range(4):
            place_q = positions[turned(way) * 4 + q] - row * 16
            is_own = (place_q >= 0) & (place_q < 16)
            crosses[part][2, q] = jnp.where(is_own, spreads[part][jnp.clip(place_q, 0, 15)], relays[part][q])
        stage2[part].append(send(crosses[part].at[2], landeds[part].at[pl.ds(4, 4)], s2s.at[s + 2], s2r.at[s + 2], turned(way) * 8 + r))

    cross(0)
    cross(1)
    cross(2)
    merge(0)
    cross(3)
    merge(1)
    g_copies[0].wait_recv()
    other_rows = gfull.at[lax.rem(other, 2) * 2 + c]
    g_copies.append(send(other_rows, other_rows, gs.at[2], gr.at[2], sibling))
    merge(2)
    merge(3)

    g_copies[1].wait_recv()
    g_copies[2].wait_recv()
    g = gfull[...].reshape(WIDTH, WIDTH)

    @pl.when(c == 0)
    def _():
        stat[...] = lax.dot_general(g, g, (((1,), (1,)), ((), ())), preferred_element_type=F32)

    @pl.when(c == 1)
    def _():
        stat[...] = lax.dot_general(g.T, g, (((1,), (0,)), ((), ())), preferred_element_type=F32)

    mine = row * 4 + lax.div(x, 2) * 2 + c
    outer = lax.rem(x + 3 + 2 * lax.rem(x, 2), 4)
    back1 = []
    for (part, at), piece in zip(BACK_SPOT, packed(stat)):
        stat_packs[part][:, at] = piece
    for part in range(BACKS):
        stat_alls[part][mine] = stat_packs[part][r]
        copies = []
        for s, (to_x, to_c) in enumerate([(x, 1 - c), (outer, c), (outer, 1 - c)]):
            to, s = to_x * 2 + to_c, s + part * 3
            copies.append(send(stat_packs[part].at[to], stat_alls[part].at[mine], r1s.at[s], r1r.at[s], row * 8 + to))
        back1.append(copies)

    stage3 = []
    back2 = []
    for part in range(PARTS):
        stage2[part][1].wait_recv()
        stage2[part][2].wait_recv()
        for q in range(4):
            origin = lax.div(positions[row * 4 + q], 16)
            t = lax.rem(row - origin + 4, 4) if ways[part] == 1 else lax.rem(origin - row + 4, 4)
            chosens[part][q] = landeds[part][jnp.where(t >= 2, t - 1, t) * 4 + q]
        copies = []
        for t in range(1, ROWS):
            peer = row_peer(t)
            q = lax.div(peer, 4) * 2 + lax.rem(peer, 2)
            s = part * 7 + t - 1
            copies.append(send(chosens[part].at[q], factors[part].at[r], s3s.at[s], s3r.at[s], row * 8 + peer))
        factors[part][r] = chosens[part][lax.div(x, 2) * 2 + c]
        stage3.append(copies)

        if part == 0:
            for back, way in enumerate(back_ways):
                for copy in back1[back]:
                    copy.wait_recv()
                here = stat_alls[back].at[pl.ds(4 * row, 4)]
                s = back * 3
                copies = []
                for t, by in enumerate((way, 4 - way)):
                    copies.append(send(here, here, r2s.at[s + t], r2r.at[s + t], turned(by) * 8 + r))
                back2.append(copies)

    sent(stage1 + stage2 + back1 + [g_copies])

    norm = jnp.zeros((TILE, TILE), F32)
    def arrived(n):
        part, at = SPOT[n]
        if part not in here:
            here.append(part)
            for copy in stage3[part]:
                copy.wait_recv()
        return factors[part][:, at].reshape(TILE, TILE).astype(F32)

    here = []
    for i, j, old in unpacked(arrived):
        mixed = BETA * old + (1.0 - BETA) * block(stat, i, j)
        m_ref[i * TILE:(i + 1) * TILE, j * TILE:(j + 1) * TILE] = mixed
        if i == j:
            norm = norm + mixed * mixed
        else:
            m_ref[j * TILE:(j + 1) * TILE, i * TILE:(i + 1) * TILE] = mixed.T
            norm = norm + 2.0 * (mixed * mixed)
    total = jnp.sum(jnp.sum(norm, axis=0, keepdims=True), axis=1, keepdims=True)
    scale = jnp.sqrt(total + EPS)
    inverse_scale = 1.0 / scale
    start = lax.rsqrt(jnp.sqrt(scale))

    further = []
    for part, way in enumerate(back_ways):
        here = stat_alls[part].at[pl.ds(4 * turned(4 - way), 4)]
        s = part * 3 + 2
        further.append(pltpu.make_async_remote_copy(
            src_ref=here, dst_ref=here, send_sem=r2s.at[s], recv_sem=r2r.at[s],
            device_id=(turned(way) * 8 + r, mp), device_id_type=MESH,
        ))

    HALF = WIDTH // 2
    halves = [pl.ds(h * HALF, HALF) for h in range(2)]
    for h, rows in enumerate(halves):
        reduced = m_ref[rows] * inverse_scale
        m_ref[rows] = reduced
        b_ref[rows] = reduced.astype(BF)
        at = lax.broadcasted_iota(jnp.int32, (HALF, WIDTH), 0) + h * HALF
        eye = at == lax.broadcasted_iota(jnp.int32, (HALF, WIDTH), 1)
        x_ref[rows] = jnp.where(eye, start, 0.0)

    def dot(a, b):
        return jnp.dot(a, b, preferred_element_type=F32)

    def apply(cols):
        return 1.25 * x_ref[:, cols] - 0.25 * dot(xl_ref[...], b_ref[:, cols])

    def step(index, carry):
        @pl.when(index == 2)
        def _():
            for part in range(BACKS):
                back2[part][0].wait_recv()
                further[part].start()

        xl_ref[...] = x_ref[...].astype(BF)
        for cols in halves:
            p_ref[:, cols] = (dot(b_ref[...], b_ref[:, cols]) * 0.0625 - 0.625 * b_ref[:, cols].astype(F32)).astype(BF)
        x_ref[:, halves[0]] = apply(halves[0])
        for cols in halves:
            f_ref[:, cols] = (dot(p_ref[...], p_ref[:, cols]) + 3.125 * p_ref[:, cols].astype(F32)).astype(BF)
        x_ref[:, halves[1]] = apply(halves[1])
        for cols in halves:
            after = 2.44140625 * m_ref[:, cols] + dot(f_ref[...], b_ref[:, cols])
            m_ref[:, cols] = after
            b_ref[:, cols] = after.astype(BF)
        return carry

    lax.fori_loop(0, ITERS - 1, step, 0)
    for part in range(BACKS):
        back2[part].append(further[part])

    for copies in back2:
        copies[1].wait_recv()
        copies[2].wait_recv()
    back3 = []
    for part in range(BACKS):
        for t in range(1, ROWS):
            peer = row_peer(t)
            for k in range(2):
                stat_picks[part][t - 1, k] = stat_alls[part][jnp.maximum(inverse[2 * peer + k], 0)]
            s = part * 7 + t - 1
            back3.append(send(stat_picks[part].at[t - 1], stat_backs[part].at[r], r3s.at[s], r3r.at[s], row * 8 + peer))
        for k in range(2):
            stat_backs[part][r, k] = stat_alls[part][jnp.maximum(inverse[2 * r + k], 0)]

    root_copies = []
    xl_ref[...] = x_ref[...].astype(BF)
    for h, cols in enumerate(halves):
        roots[c, :, cols] = apply(cols).astype(BF)
        here = roots.at[c, :, cols]
        root_copies.append(send(here, here, rts.at[h], rtr.at[h], sibling))

    for copy in root_copies:
        copy.wait_recv()
    left = roots[0, pl.ds(quad * TILE, TILE)]
    first = dot(left, gfull[...].reshape(WIDTH, WIDTH)).astype(BF)
    raw = dot(first, roots[1])
    raw_ref[...] = raw
    raw_sum = jnp.sum(raw * raw, axis=0, keepdims=True)
    raw_sum = raw_sum[:, :128] + raw_sum[:, 128:256] + raw_sum[:, 256:384] + raw_sum[:, 384:]

    v = row * 4 + zlo * 2 + c
    sums_a[v, :, :128] = grad_sum
    sums_a[v, :, 128:] = raw_sum
    round_a = []
    for s, d in enumerate(column):
        dp, to_mp = column_peer(*d)
        round_a.append(send(sums_a.at[v], sums_a.at[v], pas.at[s], par.at[s], dp, to_mp))
    sent(stage3 + back2 + [root_copies])
    for copy in round_a:
        copy.wait_recv()
    u = x * 4 + y
    sums_b[u] = jnp.sum(sums_a[...], axis=0)
    round_b = []
    for s, d in enumerate(plane):
        dp, to_mp = plane_peer(*d)
        round_b.append(send(sums_b.at[u], sums_b.at[u], pbs.at[s], pbr.at[s], dp, to_mp))

    sent([round_a, back3, round_b])

    for copy in back3:
        copy.wait_recv()
    stores = []
    for k in range(2):
        present = inverse[2 * r + k] >= 0

        def returned(n):
            part, at = BACK_SPOT[n]
            return stat_backs[part][:, k, at].reshape(TILE, TILE).astype(F32)

        for i, j, got in unpacked(returned):
            for a, b, value in ((i, j, got),) + (((j, i, got.T),) if i != j else ()):
                old = state[k, a * TILE:(a + 1) * TILE, b * TILE:(b + 1) * TILE]
                state[k, a * TILE:(a + 1) * TILE, b * TILE:(b + 1) * TILE] = jnp.where(
                    present, BETA * old + (1.0 - BETA) * value, old
                )
        store = pltpu.make_async_copy(state.at[k], new_hbm.at[k], loc.at[k])
        store.start()
        stores.append(store)

    for copy in round_b:
        copy.wait_recv()
    both = jnp.sum(sums_b[...], axis=0)
    grad_total = jnp.sum(both[:, :128], axis=1, keepdims=True)
    raw_total = jnp.sum(both[:, 128:], axis=1, keepdims=True)
    ratio = jnp.sqrt(grad_total / (raw_total + EPS))
    update[...] = (raw_ref[...] * ratio).astype(BF)

    for store in stores:
        store.wait()


def shards(grad, stat_state, owners):
    dma = pltpu.SemaphoreType.DMA
    vm = pltpu.VMEM

    def parted(*shape):
        return [vm(shape + (size, 16, TILE), BF) for size in SIZES]

    def backed(*shape):
        return [vm(shape + (size, 16, TILE), BF) for size in BACK_SIZES]

    sems = []
    for count in (7 * PARTS, 3 * PARTS, 7 * PARTS, 3, 3 * BACKS, 3 * BACKS, 7 * BACKS, 2, 15, 15):
        sems += [dma((count,)), dma((count,))]
    square = (WIDTH, WIDTH)
    results = pl.pallas_call(
        kernel,
        out_shape=(
            jax.ShapeDtypeStruct((TILE, WIDTH), BF),
            jax.ShapeDtypeStruct((2, WIDTH, WIDTH), F32),
        ),
        in_specs=[
            pl.BlockSpec(memory_space=pltpu.HBM),
            pl.BlockSpec(memory_space=pltpu.HBM),
            pl.BlockSpec(memory_space=pltpu.HBM),
        ],
        out_specs=(pl.BlockSpec(memory_space=pltpu.VMEM), pl.BlockSpec(memory_space=pl.ANY)),
        scratch_shapes=[
            vm((2, WIDTH, WIDTH), F32),
            pltpu.SMEM((1, COUNT), jnp.int32),
            pltpu.SMEM((COUNT,), jnp.int32),
            pltpu.SMEM((COUNT,), jnp.int32),
            parted(ROWS, 2), parted(16), parted(3, 4), parted(4), parted(12), parted(4), parted(ROWS),
            backed(ROWS), backed(COUNT), backed(7, 2), backed(ROWS, 2),
            vm((4, TILE, WIDTH), BF),
            vm(square, F32),
            vm(square, F32), vm(square, F32), vm(square, BF), vm(square, BF), vm(square, BF), vm(square, BF),
            vm((2, WIDTH, WIDTH), BF),
            vm((TILE, WIDTH), F32),
            vm((16, 1, 256), F32),
            vm((16, 1, 256), F32),
            *sems,
            dma((4,)),
        ],
        compiler_params=pltpu.CompilerParams(
            collective_id=0, has_side_effects=True, vmem_limit_bytes=60 * 1024 * 1024
        ),
    )(owners, grad, stat_state)
    hbm = pl.BlockSpec(memory_space=pltpu.HBM)
    return pl.pallas_call(
        hand_over,
        out_shape=tuple(jax.ShapeDtypeStruct(a.shape, a.dtype) for a in results),
        in_specs=[hbm, hbm],
        out_specs=(hbm, hbm),
        scratch_shapes=[vm((2, WIDTH, WIDTH), F32), vm((TILE, WIDTH), BF), dma((2, 9))],
        compiler_params=pltpu.CompilerParams(vmem_limit_bytes=60 * 1024 * 1024),
    )(*results)


def hand_over(update, new, update_out, new_out, held, held_update, sems):
    ways = [(update, held_update, update_out)]
    for s in range(8):
        rows = pl.ds(s % 4 * TILE, TILE)
        ways.append((new.at[s // 4, rows], held.at[s // 4, rows], new_out.at[s // 4, rows]))
    into = [pltpu.make_async_copy(a, b, sems.at[0, s]) for s, (a, b, _) in enumerate(ways)]
    out = [pltpu.make_async_copy(b, c, sems.at[1, s]) for s, (_, b, c) in enumerate(ways)]
    for copy in into:
        copy.start()
    for copy, then in zip(into, out):
        copy.wait()
        then.start()
    for copy in out:
        copy.wait()


def solution(mesh):
    return jax.shard_map(
        shards,
        mesh=mesh,
        in_specs=(P("dp", "mp"), P("dp", "mp", None), P("mp", None)),
        out_specs=(P("dp", "mp"), P("dp", "mp", None)),
        check_vma=False,
    )
```

```python
import jax
import jax.numpy as jnp
from jax import lax
from jax.experimental import pallas as pl
from jax.experimental.pallas import tpu as pltpu
from jax.sharding import PartitionSpec as P

ITERS = 6
BETA = 0.9
EPS = 1e-06
MESH = pl.DeviceIdType.MESH
BF = jnp.bfloat16
F32 = jnp.float32

WIDTH = 512
TILE = 128
COUNT = 16
ROWS = 8
PAIRS = [(i, j) for i in range(4) for j in range(i + 1, 4)]
SIZES = (5, 4)
PARTS = len(SIZES)
SPOT = [(p, n) for p, size in enumerate(SIZES) for n in range(size)]
BLOCKS = sum(SIZES)


def block(ref, i, j):
    return ref[i * TILE:(i + 1) * TILE, j * TILE:(j + 1) * TILE]


def packed(ref):
    half = TILE // 2
    diag = [block(ref, d, d) for d in range(4)]
    upper = [jnp.concatenate([diag[d][:half], diag[d + 1][:half]], axis=0) for d in (0, 2)]
    left = lax.broadcasted_iota(jnp.int32, (half, TILE), 1) < half
    lower = [jnp.where(left, pltpu.roll(diag[d + 1][half:], half, 1), diag[d][half:]) for d in (0, 2)]
    blocks = upper + [jnp.concatenate(lower, axis=0)] + [block(ref, i, j) for i, j in PAIRS]
    return [b.astype(BF).reshape(ROWS, 16, TILE) for b in blocks]


def unpacked(get):
    half = TILE // 2
    low = lax.broadcasted_iota(jnp.int32, (TILE, TILE), 0) >= half
    left = lax.broadcasted_iota(jnp.int32, (TILE, TILE), 1) < half
    corners = get(2)
    for d in range(4):
        upper = get(d // 2)[d % 2 * half:(d % 2 + 1) * half]
        corner = corners[d // 2 * half:(d // 2 + 1) * half]
        if d % 2:
            corner = pltpu.roll(corner, half, 1)
        whole = jnp.concatenate([upper, corner], axis=0)
        yield d, d, jnp.where(low & left, whole.T, whole)
    for n, (i, j) in enumerate(PAIRS):
        yield i, j, get(3 + n)


def kernel(
    owners_hbm, grad, state_hbm, update, new_hbm,
    state, owners, positions, inverse,
    packs, spreads, crosses, relays, landeds, chosens, factors,
    stat_pack, stat_all, stat_pick, stat_back, gfull, stat,
    m_ref, x_ref, b_ref, p_ref, f_ref, xl_ref, roots, raw_ref, sums,
    s1s, s1r, s2s, s2r, s3s, s3r, gs, gr, r1s, r1r, r2s, r2r, r3s, r3r, rts, rtr, pas, par, loc,
):
    me = lax.axis_index("dp")
    mp = lax.axis_index("mp")
    row, r = lax.div(me, 8), lax.rem(me, 8)
    x, c = lax.div(r, 2), lax.rem(r, 2)
    quad = lax.rem(x, 2) * 2 + c

    def send(src, dst, ssem, rsem, dp, mp_to=None):
        copy = pltpu.make_async_remote_copy(
            src_ref=src, dst_ref=dst, send_sem=ssem, recv_sem=rsem,
            device_id=(dp, mp if mp_to is None else mp_to), device_id_type=MESH,
        )
        copy.start()
        return copy

    def sent(groups):
        for copies in groups:
            for copy in copies:
                copy.wait_send()

    def row_peer(t):
        return lax.rem(r + t, 8)

    def turned(by):
        return lax.rem(row + by, 4)

    in_mp = (mp, [(me, lax.rem(mp + t, 8)) for t in range(1, 8)])
    in_rows = (row, [(turned(t) * 8 + r, mp) for t in range(1, 4)])
    in_row = (r, [(row * 8 + row_peer(t), mp) for t in range(1, ROWS)])
    rounds = (in_mp, in_rows, in_row)

    loads = [pltpu.make_async_copy(state_hbm.at[k], state.at[k], loc.at[k]) for k in range(2)]
    for load in loads:
        load.start()
    own_grad = pltpu.make_async_copy(grad, gfull.at[quad], loc.at[2])
    own_grad.start()
    own_table = pltpu.make_async_copy(owners_hbm, owners, loc.at[3])
    own_table.start()
    barrier = pltpu.get_barrier_semaphore()
    greeted = in_row[1] + in_rows[1] + in_mp[1]
    for peer in greeted:
        pl.semaphore_signal(barrier, inc=1, device_id=peer, device_id_type=MESH)

    for k in range(2):
        loads[k].wait()
        for (part, at), piece in zip(SPOT, packed(state.at[k])):
            packs[part][:, k, at] = piece
    for part in range(PARTS):
        spreads[part][pl.ds(2 * r, 2)] = packs[part][r]
    pl.semaphore_wait(barrier, len(greeted))

    stage1 = []
    for part in range(PARTS):
        copies = []
        for t in range(1, ROWS):
            peer = row_peer(t)
            s = part * 7 + t - 1
            copies.append(send(packs[part].at[peer], spreads[part].at[pl.ds(2 * r, 2)], s1s.at[s], s1r.at[s], row * 8 + peer))
        stage1.append(copies)
    own_grad.wait()
    other = x + 1 - 2 * lax.rem(x, 2)
    sibling = row * 8 + x * 2 + 1 - c
    own_rows = gfull.at[quad]
    g_copies = [
        send(own_rows, own_rows, gs.at[0], gr.at[0], row * 8 + other * 2 + c),
        send(own_rows, own_rows, gs.at[1], gr.at[1], sibling),
    ]

    own_table.wait()
    table = [owners[0, f] for f in range(COUNT)]
    place = []
    for f in range(COUNT):
        slot = jnp.int32(0)
        for g in range(f):
            slot = slot + jnp.where(table[g] == table[f], 1, 0)
        place.append(table[f] * 2 + slot)
        positions[f] = place[f]

    def invert(index, carry):
        target = row * 16 + index
        found = jnp.int32(-1)
        for f in range(COUNT):
            found = jnp.where(positions[f] == target, f, found)
        inverse[index] = found
        return carry

    lax.fori_loop(0, COUNT, invert, 0)

    wide = gfull[quad].astype(F32)
    grad_sum = jnp.sum(wide * wide, axis=0, keepdims=True)
    grad_sum = grad_sum[:, :128] + grad_sum[:, 128:256] + grad_sum[:, 256:384] + grad_sum[:, 384:]

    ways = (1, 3) * (PARTS // 2)
    stage2 = []

    def cross(part):
        way = ways[part]
        for copy in stage1[part]:
            copy.wait_recv()

        def own(to_row, q):
            return spreads[part][jnp.clip(positions[to_row * 4 + q] - row * 16, 0, 15)]

        s = part * 3
        copies = []
        for q in range(4):
            crosses[part][0, q] = own(turned(2), q)
        copies.append(send(crosses[part].at[0], relays[part], s2s.at[s], s2r.at[s], turned(way) * 8 + r))
        for q in range(4):
            crosses[part][1, q] = own(turned(4 - way), q)
        copies.append(send(crosses[part].at[1], landeds[part].at[pl.ds(8, 4)], s2s.at[s + 1], s2r.at[s + 1], turned(4 - way) * 8 + r))
        for q in range(4):
            landeds[part][q] = own(row, q)
        stage2.append(copies)

    def merge(part):
        way = ways[part]
        stage2[part][0].wait_recv()
        s = part * 3
        for q in range(4):
            place_q = positions[turned(way) * 4 + q] - row * 16
            is_own = (place_q >= 0) & (place_q < 16)
            crosses[part][2, q] = jnp.where(is_own, spreads[part][jnp.clip(place_q, 0, 15)], relays[part][q])
        stage2[part].append(send(crosses[part].at[2], landeds[part].at[pl.ds(4, 4)], s2s.at[s + 2], s2r.at[s + 2], turned(way) * 8 + r))

    cross(0)
    cross(1)
    merge(0)
    g_copies[0].wait_recv()
    other_rows = gfull.at[lax.rem(other, 2) * 2 + c]
    g_copies.append(send(other_rows, other_rows, gs.at[2], gr.at[2], sibling))
    merge(1)

    g_copies[1].wait_recv()
    g_copies[2].wait_recv()
    g = gfull[...].reshape(WIDTH, WIDTH)

    @pl.when(c == 0)
    def _():
        stat[...] = lax.dot_general(g, g, (((1,), (1,)), ((), ())), preferred_element_type=F32)

    @pl.when(c == 1)
    def _():
        stat[...] = lax.dot_general(g.T, g, (((1,), (0,)), ((), ())), preferred_element_type=F32)

    mine = row * 4 + lax.div(x, 2) * 2 + c
    outer = lax.rem(x + 3 + 2 * lax.rem(x, 2), 4)
    for n, piece in enumerate(packed(stat)):
        stat_pack[:, n] = piece
    stat_all[mine] = stat_pack[r]
    back1 = []
    for s, (to_x, to_c) in enumerate([(x, 1 - c), (outer, c), (outer, 1 - c)]):
        to = to_x * 2 + to_c
        back1.append(send(stat_pack.at[to], stat_all.at[mine], r1s.at[s], r1r.at[s], row * 8 + to))

    stage3 = []
    back2 = []
    for part in range(PARTS):
        stage2[part][1].wait_recv()
        stage2[part][2].wait_recv()
        for q in range(4):
            origin = lax.div(positions[row * 4 + q], 16)
            t = lax.rem(row - origin + 4, 4) if ways[part] == 1 else lax.rem(origin - row + 4, 4)
            chosens[part][q] = landeds[part][jnp.where(t >= 2, t - 1, t) * 4 + q]
        copies = []
        for t in range(1, ROWS):
            peer = row_peer(t)
            q = lax.div(peer, 4) * 2 + lax.rem(peer, 2)
            s = part * 7 + t - 1
            copies.append(send(chosens[part].at[q], factors[part].at[r], s3s.at[s], s3r.at[s], row * 8 + peer))
        factors[part][r] = chosens[part][lax.div(x, 2) * 2 + c]
        stage3.append(copies)

        if part == 0:
            for copy in back1:
                copy.wait_recv()
            here = stat_all.at[pl.ds(4 * row, 4)]
            for s, way in enumerate(ways):
                back2.append(send(here, here, r2s.at[s], r2r.at[s], turned(way) * 8 + r))

    sent(stage1 + stage2 + [back1, g_copies])

    norm = jnp.zeros((TILE, TILE), F32)
    def arrived(n):
        part, at = SPOT[n]
        if part not in here:
            here.append(part)
            for copy in stage3[part]:
                copy.wait_recv()
        return factors[part][:, at].reshape(TILE, TILE).astype(F32)

    here = []
    for i, j, old in unpacked(arrived):
        mixed = BETA * old + (1.0 - BETA) * block(stat, i, j)
        m_ref[i * TILE:(i + 1) * TILE, j * TILE:(j + 1) * TILE] = mixed
        if i == j:
            norm = norm + mixed * mixed
        else:
            m_ref[j * TILE:(j + 1) * TILE, i * TILE:(i + 1) * TILE] = mixed.T
            norm = norm + 2.0 * (mixed * mixed)
    total = jnp.sum(jnp.sum(norm, axis=0, keepdims=True), axis=1, keepdims=True)
    scale = jnp.sqrt(total + EPS)
    inverse_scale = 1.0 / scale
    start = lax.rsqrt(jnp.sqrt(scale))

    further = []
    for part, way in enumerate(ways):
        here = stat_all.at[pl.ds(4 * turned(4 - way), 4), pl.ds(part * SIZES[0], SIZES[part])]
        further.append(pltpu.make_async_remote_copy(
            src_ref=here, dst_ref=here, send_sem=r2s.at[2 + part], recv_sem=r2r.at[2 + part],
            device_id=(turned(way) * 8 + r, mp), device_id_type=MESH,
        ))

    HALF = WIDTH // 2
    halves = [pl.ds(h * HALF, HALF) for h in range(2)]
    for h, rows in enumerate(halves):
        reduced = m_ref[rows] * inverse_scale
        m_ref[rows] = reduced
        b_ref[rows] = reduced.astype(BF)
        at = lax.broadcasted_iota(jnp.int32, (HALF, WIDTH), 0) + h * HALF
        eye = at == lax.broadcasted_iota(jnp.int32, (HALF, WIDTH), 1)
        x_ref[rows] = jnp.where(eye, start, 0.0)

    def dot(a, b):
        return jnp.dot(a, b, preferred_element_type=F32)

    def apply(cols):
        return 1.25 * x_ref[:, cols] - 0.25 * dot(xl_ref[...], b_ref[:, cols])

    def step(index, carry):
        @pl.when(index == 2)
        def _():
            for near, far in zip(back2, further):
                near.wait_recv()
                far.start()

        xl_ref[...] = x_ref[...].astype(BF)
        for cols in halves:
            p_ref[:, cols] = (dot(b_ref[...], b_ref[:, cols]) * 0.0625 - 0.625 * b_ref[:, cols].astype(F32)).astype(BF)
        x_ref[:, halves[0]] = apply(halves[0])
        for cols in halves:
            f_ref[:, cols] = (dot(p_ref[...], p_ref[:, cols]) + 3.125 * p_ref[:, cols].astype(F32)).astype(BF)
        x_ref[:, halves[1]] = apply(halves[1])
        for cols in halves:
            after = 2.44140625 * m_ref[:, cols] + dot(f_ref[...], b_ref[:, cols])
            m_ref[:, cols] = after
            b_ref[:, cols] = after.astype(BF)
        return carry

    lax.fori_loop(0, ITERS - 1, step, 0)
    for copy in further:
        copy.wait_recv()
    back3 = []
    for t in range(1, ROWS):
        peer = row_peer(t)
        for k in range(2):
            stat_pick[t - 1, k] = stat_all[jnp.maximum(inverse[2 * peer + k], 0)]
        back3.append(send(stat_pick.at[t - 1], stat_back.at[r], r3s.at[t - 1], r3r.at[t - 1], row * 8 + peer))
    for k in range(2):
        stat_back[r, k] = stat_all[jnp.maximum(inverse[2 * r + k], 0)]

    root_copies = []
    xl_ref[...] = x_ref[...].astype(BF)
    for h, cols in enumerate(halves):
        roots[c, :, cols] = apply(cols).astype(BF)
        here = roots.at[c, :, cols]
        root_copies.append(send(here, here, rts.at[h], rtr.at[h], sibling))

    for copy in root_copies:
        copy.wait_recv()
    left = roots[0, pl.ds(quad * TILE, TILE)]
    first = dot(left, gfull[...].reshape(WIDTH, WIDTH)).astype(BF)
    raw = dot(first, roots[1])
    raw_ref[...] = raw
    raw_sum = jnp.sum(raw * raw, axis=0, keepdims=True)
    raw_sum = raw_sum[:, :128] + raw_sum[:, 128:256] + raw_sum[:, 256:384] + raw_sum[:, 384:]

    def start_round(n, value):
        at, peers = rounds[n]
        sums[n][at] = value
        here = sums[n].at[at]
        base = (0, 7, 10)[n]
        return [send(here, here, pas.at[base + s], par.at[base + s], *peer) for s, peer in enumerate(peers)]

    def finish_round(n, copies):
        for copy in copies:
            copy.wait_recv()
        return jnp.sum(sums[n][...], axis=0)

    round_a = start_round(0, jnp.concatenate([grad_sum, raw_sum], axis=1))
    sent(stage3 + [back2, further, root_copies])
    round_b = start_round(1, finish_round(0, round_a))
    round_c = start_round(2, finish_round(1, round_b))
    sent([round_a, round_b, round_c, back3])

    for copy in back3:
        copy.wait_recv()
    stores = []
    for k in range(2):
        present = inverse[2 * r + k] >= 0

        def returned(n):
            return stat_back[:, k, n].reshape(TILE, TILE).astype(F32)

        for i, j, got in unpacked(returned):
            for a, b, value in ((i, j, got),) + (((j, i, got.T),) if i != j else ()):
                old = state[k, a * TILE:(a + 1) * TILE, b * TILE:(b + 1) * TILE]
                state[k, a * TILE:(a + 1) * TILE, b * TILE:(b + 1) * TILE] = jnp.where(
                    present, BETA * old + (1.0 - BETA) * value, old
                )
        store = pltpu.make_async_copy(state.at[k], new_hbm.at[k], loc.at[k])
        store.start()
        stores.append(store)

    both = finish_round(2, round_c)
    grad_total = jnp.sum(both[:, :128], axis=1, keepdims=True)
    raw_total = jnp.sum(both[:, 128:], axis=1, keepdims=True)
    ratio = jnp.sqrt(grad_total / (raw_total + EPS))
    update[...] = (raw_ref[...] * ratio).astype(BF)

    for store in stores:
        store.wait()


def shards(grad, stat_state, owners):
    dma = pltpu.SemaphoreType.DMA
    vm = pltpu.VMEM

    def parted(*shape):
        return [vm(shape + (size, 16, TILE), BF) for size in SIZES]

    sems = []
    for count in (7 * PARTS, 3 * PARTS, 7 * PARTS, 3, 3, 4, 7, 2, 17):
        sems += [dma((count,)), dma((count,))]
    square = (WIDTH, WIDTH)
    results = pl.pallas_call(
        kernel,
        out_shape=(
            jax.ShapeDtypeStruct((TILE, WIDTH), BF),
            jax.ShapeDtypeStruct((2, WIDTH, WIDTH), F32),
        ),
        in_specs=[
            pl.BlockSpec(memory_space=pltpu.HBM),
            pl.BlockSpec(memory_space=pltpu.HBM),
            pl.BlockSpec(memory_space=pltpu.HBM),
        ],
        out_specs=(pl.BlockSpec(memory_space=pltpu.VMEM), pl.BlockSpec(memory_space=pl.ANY)),
        scratch_shapes=[
            vm((2, WIDTH, WIDTH), F32),
            pltpu.SMEM((1, COUNT), jnp.int32),
            pltpu.SMEM((COUNT,), jnp.int32),
            pltpu.SMEM((COUNT,), jnp.int32),
            parted(ROWS, 2), parted(16), parted(3, 4), parted(4), parted(12), parted(4), parted(ROWS),
            vm((ROWS, BLOCKS, 16, TILE), BF),
            vm((COUNT, BLOCKS, 16, TILE), BF),
            vm((7, 2, BLOCKS, 16, TILE), BF),
            vm((ROWS, 2, BLOCKS, 16, TILE), BF),
            vm((4, TILE, WIDTH), BF),
            vm(square, F32),
            vm(square, F32), vm(square, F32), vm(square, BF), vm(square, BF), vm(square, BF), vm(square, BF),
            vm((2, WIDTH, WIDTH), BF),
            vm((TILE, WIDTH), F32),
            [vm((n, 1, 256), F32) for n in (8, 4, 8)],
            *sems,
            dma((4,)),
        ],
        compiler_params=pltpu.CompilerParams(
            collective_id=0, has_side_effects=True, vmem_limit_bytes=60 * 1024 * 1024
        ),
    )(owners, grad, stat_state)
    hbm = pl.BlockSpec(memory_space=pltpu.HBM)
    return pl.pallas_call(
        hand_over,
        out_shape=tuple(jax.ShapeDtypeStruct(a.shape, a.dtype) for a in results),
        in_specs=[hbm, hbm],
        out_specs=(hbm, hbm),
        scratch_shapes=[vm((2, WIDTH, WIDTH), F32), vm((TILE, WIDTH), BF), dma((2, 9))],
        compiler_params=pltpu.CompilerParams(vmem_limit_bytes=60 * 1024 * 1024),
    )(*results)


def hand_over(update, new, update_out, new_out, held, held_update, sems):
    ways = [(update, held_update, update_out)]
    for s in range(8):
        rows = pl.ds(s % 4 * TILE, TILE)
        ways.append((new.at[s // 4, rows], held.at[s // 4, rows], new_out.at[s // 4, rows]))
    into = [pltpu.make_async_copy(a, b, sems.at[0, s]) for s, (a, b, _) in enumerate(ways)]
    out = [pltpu.make_async_copy(b, c, sems.at[1, s]) for s, (_, b, c) in enumerate(ways)]
    for copy in into:
        copy.start()
    for copy, then in zip(into, out):
        copy.wait()
        then.start()
    for copy in out:
        copy.wait()


def solution(mesh):
    return jax.shard_map(
        shards,
        mesh=mesh,
        in_specs=(P("dp", "mp"), P("dp", "mp", None), P("mp", None)),
        out_specs=(P("dp", "mp"), P("dp", "mp", None)),
        check_vma=False,
    )
```

```python
import jax
import jax.numpy as jnp
from jax import lax
from jax.experimental import pallas as pl
from jax.experimental.pallas import tpu as pltpu
from jax.sharding import PartitionSpec as P

ITERS = 6
BETA = 0.9
EPS = 1e-06
MESH = pl.DeviceIdType.MESH
BF = jnp.bfloat16
F32 = jnp.float32

WIDTH = 512
TILE = 128
COUNT = 16
ROWS = 8
PAIRS = [(i, j) for i in range(4) for j in range(i + 1, 4)]
SIZES = (5, 4)
PARTS = len(SIZES)
SPOT = [(p, n) for p, size in enumerate(SIZES) for n in range(size)]
BLOCKS = sum(SIZES)


def block(ref, i, j):
    return ref[i * TILE:(i + 1) * TILE, j * TILE:(j + 1) * TILE]


def packed(ref):
    half = TILE // 2
    diag = [block(ref, d, d) for d in range(4)]
    upper = [jnp.concatenate([diag[d][:half], diag[d + 1][:half]], axis=0) for d in (0, 2)]
    left = lax.broadcasted_iota(jnp.int32, (half, TILE), 1) < half
    lower = [jnp.where(left, pltpu.roll(diag[d + 1][half:], half, 1), diag[d][half:]) for d in (0, 2)]
    blocks = upper + [jnp.concatenate(lower, axis=0)] + [block(ref, i, j) for i, j in PAIRS]
    return [b.astype(BF).reshape(ROWS, 16, TILE) for b in blocks]


def unpacked(get):
    half = TILE // 2
    low = lax.broadcasted_iota(jnp.int32, (TILE, TILE), 0) >= half
    left = lax.broadcasted_iota(jnp.int32, (TILE, TILE), 1) < half
    corners = get(2)
    for d in range(4):
        upper = get(d // 2)[d % 2 * half:(d % 2 + 1) * half]
        corner = corners[d // 2 * half:(d // 2 + 1) * half]
        if d % 2:
            corner = pltpu.roll(corner, half, 1)
        whole = jnp.concatenate([upper, corner], axis=0)
        yield d, d, jnp.where(low & left, whole.T, whole)
    for n, (i, j) in enumerate(PAIRS):
        yield i, j, get(3 + n)


def kernel(
    owners_hbm, grad, state_hbm, update, new_hbm,
    state, owners, positions, inverse,
    packs, spreads, crosses, relays, landeds, chosens, factors,
    stat_pack, stat_all, stat_pick, stat_back, gfull, stat,
    m_ref, x_ref, b_ref, p_ref, f_ref, xl_ref, roots, raw_ref, sums,
    s1s, s1r, s2s, s2r, s3s, s3r, gs, gr, r1s, r1r, r2s, r2r, r3s, r3r, rts, rtr, pas, par, loc,
):
    me = lax.axis_index("dp")
    mp = lax.axis_index("mp")
    row, r = lax.div(me, 8), lax.rem(me, 8)
    x, c = lax.div(r, 2), lax.rem(r, 2)
    quad = lax.rem(x, 2) * 2 + c

    def remote(src, dst, ssem, rsem, dp, mp_to=None):
        return pltpu.make_async_remote_copy(
            src_ref=src, dst_ref=dst, send_sem=ssem, recv_sem=rsem,
            device_id=(dp, mp if mp_to is None else mp_to), device_id_type=MESH,
        )

    def send(*args):
        copy = remote(*args)
        copy.start()
        return copy

    def sent(groups):
        for copies in groups:
            for copy in copies:
                copy.wait_send()

    def row_peer(t):
        return lax.rem(r + t, 8)

    def turned(by):
        return lax.rem(row + by, 4)

    zlo, y = lax.div(mp, 4), lax.rem(mp, 4)

    def plane_peer(dx, dy):
        return row * 8 + lax.rem(x + dx, 4) * 2 + c, zlo * 4 + lax.rem(y + dy, 4)

    def column_peer(dh, dl, dc):
        return turned(dh) * 8 + x * 2 + lax.rem(c + dc, 2), lax.rem(zlo + dl, 2) * 4 + y

    plane = [(dx, dy) for dx in range(4) for dy in range(4) if dx or dy]
    column = [(dh, dl, dc) for dh in range(4) for dl in range(2) for dc in range(2) if dh or dl or dc]
    rounds = (
        (row * 4 + zlo * 2 + c, [column_peer(*d) for d in column]),
        (x * 4 + y, [plane_peer(*d) for d in plane]),
    )

    loads = [pltpu.make_async_copy(state_hbm.at[k], state.at[k], loc.at[k]) for k in range(2)]
    for load in loads:
        load.start()
    own_grad = pltpu.make_async_copy(grad, gfull.at[quad], loc.at[2])
    own_grad.start()
    own_table = pltpu.make_async_copy(owners_hbm, owners, loc.at[3])
    own_table.start()
    barrier = pltpu.get_barrier_semaphore()
    greeted = [(row * 8 + row_peer(t), mp) for t in range(1, ROWS)]
    greeted += [column_peer(*d) for d in column if d[0] or d[1]]
    greeted += [plane_peer(*d) for d in plane if d[1]]
    for peer in greeted:
        pl.semaphore_signal(barrier, inc=1, device_id=peer, device_id_type=MESH)

    for k in range(2):
        loads[k].wait()
        for (part, at), piece in zip(SPOT, packed(state.at[k])):
            packs[part][:, k, at] = piece
    for part in range(PARTS):
        spreads[part][pl.ds(2 * r, 2)] = packs[part][r]
    pl.semaphore_wait(barrier, len(greeted))

    stage1 = []
    for part in range(PARTS):
        copies = []
        for t in range(1, ROWS):
            peer = row_peer(t)
            s = part * 7 + t - 1
            copies.append(send(packs[part].at[peer], spreads[part].at[pl.ds(2 * r, 2)], s1s.at[s], s1r.at[s], row * 8 + peer))
        stage1.append(copies)
    own_grad.wait()
    other = x + 1 - 2 * lax.rem(x, 2)
    sibling = row * 8 + x * 2 + 1 - c
    own_rows = gfull.at[quad]
    g_copies = [
        send(own_rows, own_rows, gs.at[0], gr.at[0], row * 8 + other * 2 + c),
        send(own_rows, own_rows, gs.at[1], gr.at[1], sibling),
    ]

    own_table.wait()
    table = [owners[0, f] for f in range(COUNT)]
    place = []
    for f in range(COUNT):
        slot = jnp.int32(0)
        for g in range(f):
            slot = slot + jnp.where(table[g] == table[f], 1, 0)
        place.append(table[f] * 2 + slot)
        positions[f] = place[f]

    def invert(index, carry):
        target = row * 16 + index
        found = jnp.int32(-1)
        for f in range(COUNT):
            found = jnp.where(positions[f] == target, f, found)
        inverse[index] = found
        return carry

    lax.fori_loop(0, COUNT, invert, 0)

    wide = gfull[quad].astype(F32)
    grad_sum = jnp.sum(wide * wide, axis=0, keepdims=True)
    grad_sum = grad_sum[:, :128] + grad_sum[:, 128:256] + grad_sum[:, 256:384] + grad_sum[:, 384:]

    ways = (1, 3) * (PARTS // 2)
    stage2 = []

    def cross(part):
        way = ways[part]
        for copy in stage1[part]:
            copy.wait_recv()

        def own(to_row, q):
            return spreads[part][jnp.clip(positions[to_row * 4 + q] - row * 16, 0, 15)]

        s = part * 3
        copies = []
        for q in range(4):
            crosses[part][0, q] = own(turned(2), q)
        copies.append(send(crosses[part].at[0], relays[part], s2s.at[s], s2r.at[s], turned(way) * 8 + r))
        for q in range(4):
            crosses[part][1, q] = own(turned(4 - way), q)
        copies.append(send(crosses[part].at[1], landeds[part].at[pl.ds(8, 4)], s2s.at[s + 1], s2r.at[s + 1], turned(4 - way) * 8 + r))
        for q in range(4):
            landeds[part][q] = own(row, q)
        stage2.append(copies)

    def merge(part):
        way = ways[part]
        stage2[part][0].wait_recv()
        s = part * 3
        for q in range(4):
            place_q = positions[turned(way) * 4 + q] - row * 16
            is_own = (place_q >= 0) & (place_q < 16)
            crosses[part][2, q] = jnp.where(is_own, spreads[part][jnp.clip(place_q, 0, 15)], relays[part][q])
        stage2[part].append(send(crosses[part].at[2], landeds[part].at[pl.ds(4, 4)], s2s.at[s + 2], s2r.at[s + 2], turned(way) * 8 + r))

    cross(0)
    cross(1)
    merge(0)
    g_copies[0].wait_recv()
    other_rows = gfull.at[lax.rem(other, 2) * 2 + c]
    g_copies.append(send(other_rows, other_rows, gs.at[2], gr.at[2], sibling))
    merge(1)

    g_copies[1].wait_recv()
    g_copies[2].wait_recv()
    g = gfull[...].reshape(WIDTH, WIDTH)

    @pl.when(c == 0)
    def _():
        stat[...] = lax.dot_general(g, g, (((1,), (1,)), ((), ())), preferred_element_type=F32)

    @pl.when(c == 1)
    def _():
        stat[...] = lax.dot_general(g.T, g, (((1,), (0,)), ((), ())), preferred_element_type=F32)

    mine = row * 4 + lax.div(x, 2) * 2 + c
    outer = lax.rem(x + 3 + 2 * lax.rem(x, 2), 4)
    for n, piece in enumerate(packed(stat)):
        stat_pack[:, n] = piece
    stat_all[mine] = stat_pack[r]
    back1 = []
    for s, (to_x, to_c) in enumerate([(x, 1 - c), (outer, c), (outer, 1 - c)]):
        to = to_x * 2 + to_c
        back1.append(send(stat_pack.at[to], stat_all.at[mine], r1s.at[s], r1r.at[s], row * 8 + to))

    stage3 = []
    back2 = []
    for part in range(PARTS):
        stage2[part][1].wait_recv()
        stage2[part][2].wait_recv()
        for q in range(4):
            origin = lax.div(positions[row * 4 + q], 16)
            t = lax.rem(row - origin + 4, 4) if ways[part] == 1 else lax.rem(origin - row + 4, 4)
            chosens[part][q] = landeds[part][jnp.where(t >= 2, t - 1, t) * 4 + q]
        copies = []
        for t in range(1, ROWS):
            peer = row_peer(t)
            q = lax.div(peer, 4) * 2 + lax.rem(peer, 2)
            s = part * 7 + t - 1
            copies.append(send(chosens[part].at[q], factors[part].at[r], s3s.at[s], s3r.at[s], row * 8 + peer))
        factors[part][r] = chosens[part][lax.div(x, 2) * 2 + c]
        stage3.append(copies)

        if part == 0:
            for copy in back1:
                copy.wait_recv()
            here = stat_all.at[pl.ds(4 * row, 4)]
            for s, way in enumerate(ways):
                back2.append(send(here, here, r2s.at[s], r2r.at[s], turned(way) * 8 + r))

    sent(stage1 + stage2 + [back1, g_copies])

    norm = jnp.zeros((TILE, TILE), F32)
    def arrived(n):
        part, at = SPOT[n]
        if part not in here:
            here.append(part)
            for copy in stage3[part]:
                copy.wait_recv()
        return factors[part][:, at].reshape(TILE, TILE).astype(F32)

    here = []
    for i, j, old in unpacked(arrived):
        mixed = BETA * old + (1.0 - BETA) * block(stat, i, j)
        m_ref[i * TILE:(i + 1) * TILE, j * TILE:(j + 1) * TILE] = mixed
        if i == j:
            norm = norm + mixed * mixed
        else:
            m_ref[j * TILE:(j + 1) * TILE, i * TILE:(i + 1) * TILE] = mixed.T
            norm = norm + 2.0 * (mixed * mixed)
    total = jnp.sum(jnp.sum(norm, axis=0, keepdims=True), axis=1, keepdims=True)
    scale = jnp.sqrt(total + EPS)
    inverse_scale = 1.0 / scale
    start = lax.rsqrt(jnp.sqrt(scale))

    further = []
    for part, way in enumerate(ways):
        here = stat_all.at[pl.ds(4 * turned(4 - way), 4), pl.ds(part * SIZES[0], SIZES[part])]
        further.append(remote(here, here, r2s.at[2 + part], r2r.at[2 + part], turned(way) * 8 + r))
    back3 = []
    for t in range(1, ROWS):
        back3.append(remote(stat_pick.at[t - 1], stat_back.at[r], r3s.at[t - 1], r3r.at[t - 1], row * 8 + row_peer(t)))

    def hand_out():
        for copy in further:
            copy.wait_recv()
        for t in range(1, ROWS):
            for k in range(2):
                stat_pick[t - 1, k] = stat_all[jnp.maximum(inverse[2 * row_peer(t) + k], 0)]
            back3[t - 1].start()
        for k in range(2):
            stat_back[r, k] = stat_all[jnp.maximum(inverse[2 * r + k], 0)]

    HALF = WIDTH // 2
    halves = [pl.ds(h * HALF, HALF) for h in range(2)]
    for h, rows in enumerate(halves):
        reduced = m_ref[rows] * inverse_scale
        m_ref[rows] = reduced
        b_ref[rows] = reduced.astype(BF)
        at = lax.broadcasted_iota(jnp.int32, (HALF, WIDTH), 0) + h * HALF
        eye = at == lax.broadcasted_iota(jnp.int32, (HALF, WIDTH), 1)
        x_ref[rows] = jnp.where(eye, start, 0.0)

    def dot(a, b):
        return jnp.dot(a, b, preferred_element_type=F32)

    def apply(cols):
        return 1.25 * x_ref[:, cols] - 0.25 * dot(xl_ref[...], b_ref[:, cols])

    def step(index, carry):
        @pl.when(index == 2)
        def _():
            for near, far in zip(back2, further):
                near.wait_recv()
                far.start()

        pl.when(index == 4)(hand_out)

        xl_ref[...] = x_ref[...].astype(BF)
        for cols in halves:
            p_ref[:, cols] = (dot(b_ref[...], b_ref[:, cols]) * 0.0625 - 0.625 * b_ref[:, cols].astype(F32)).astype(BF)
        x_ref[:, halves[0]] = apply(halves[0])
        for cols in halves:
            f_ref[:, cols] = (dot(p_ref[...], p_ref[:, cols]) + 3.125 * p_ref[:, cols].astype(F32)).astype(BF)
        x_ref[:, halves[1]] = apply(halves[1])
        for cols in halves:
            after = 2.44140625 * m_ref[:, cols] + dot(f_ref[...], b_ref[:, cols])
            m_ref[:, cols] = after
            b_ref[:, cols] = after.astype(BF)
        return carry

    lax.fori_loop(0, ITERS - 1, step, 0)
    root_copies = []
    xl_ref[...] = x_ref[...].astype(BF)
    for h, cols in enumerate(halves):
        roots[c, :, cols] = apply(cols).astype(BF)
        here = roots.at[c, :, cols]
        root_copies.append(send(here, here, rts.at[h], rtr.at[h], sibling))

    for copy in root_copies:
        copy.wait_recv()
    left = roots[0, pl.ds(quad * TILE, TILE)]
    first = dot(left, gfull[...].reshape(WIDTH, WIDTH)).astype(BF)
    raw = dot(first, roots[1])
    raw_ref[...] = raw
    raw_sum = jnp.sum(raw * raw, axis=0, keepdims=True)
    raw_sum = raw_sum[:, :128] + raw_sum[:, 128:256] + raw_sum[:, 256:384] + raw_sum[:, 384:]

    def start_round(n, value):
        at, peers = rounds[n]
        sums[n][at] = value
        here = sums[n].at[at]
        return [send(here, here, pas.at[15 * n + s], par.at[15 * n + s], *peer) for s, peer in enumerate(peers)]

    def finish_round(n, copies):
        for copy in copies:
            copy.wait_recv()
        return jnp.sum(sums[n][...], axis=0)

    round_a = start_round(0, jnp.concatenate([grad_sum, raw_sum], axis=1))
    sent(stage3 + [back2, further, root_copies])
    round_b = start_round(1, finish_round(0, round_a))

    for copy in back3:
        copy.wait_recv()
    stores = []
    for k in range(2):
        present = inverse[2 * r + k] >= 0

        def returned(n):
            return stat_back[:, k, n].reshape(TILE, TILE).astype(F32)

        for i, j, got in unpacked(returned):
            for a, b, value in ((i, j, got),) + (((j, i, got.T),) if i != j else ()):
                old = state[k, a * TILE:(a + 1) * TILE, b * TILE:(b + 1) * TILE]
                state[k, a * TILE:(a + 1) * TILE, b * TILE:(b + 1) * TILE] = jnp.where(
                    present, BETA * old + (1.0 - BETA) * value, old
                )
        store = pltpu.make_async_copy(state.at[k], new_hbm.at[k], loc.at[k])
        store.start()
        stores.append(store)

    sent([round_a, round_b, back3])
    both = finish_round(1, round_b)
    grad_total = jnp.sum(both[:, :128], axis=1, keepdims=True)
    raw_total = jnp.sum(both[:, 128:], axis=1, keepdims=True)
    ratio = jnp.sqrt(grad_total / (raw_total + EPS))
    update[...] = (raw_ref[...] * ratio).astype(BF)

    for store in stores:
        store.wait()


def shards(grad, stat_state, owners):
    dma = pltpu.SemaphoreType.DMA
    vm = pltpu.VMEM

    def parted(*shape):
        return [vm(shape + (size, 16, TILE), BF) for size in SIZES]

    sems = []
    for count in (7 * PARTS, 3 * PARTS, 7 * PARTS, 3, 3, 4, 7, 2, 30):
        sems += [dma((count,)), dma((count,))]
    square = (WIDTH, WIDTH)
    results = pl.pallas_call(
        kernel,
        out_shape=(
            jax.ShapeDtypeStruct((TILE, WIDTH), BF),
            jax.ShapeDtypeStruct((2, WIDTH, WIDTH), F32),
        ),
        in_specs=[
            pl.BlockSpec(memory_space=pltpu.HBM),
            pl.BlockSpec(memory_space=pltpu.HBM),
            pl.BlockSpec(memory_space=pltpu.HBM),
        ],
        out_specs=(pl.BlockSpec(memory_space=pltpu.VMEM), pl.BlockSpec(memory_space=pl.ANY)),
        scratch_shapes=[
            vm((2, WIDTH, WIDTH), F32),
            pltpu.SMEM((1, COUNT), jnp.int32),
            pltpu.SMEM((COUNT,), jnp.int32),
            pltpu.SMEM((COUNT,), jnp.int32),
            parted(ROWS, 2), parted(16), parted(3, 4), parted(4), parted(12), parted(4), parted(ROWS),
            vm((ROWS, BLOCKS, 16, TILE), BF),
            vm((COUNT, BLOCKS, 16, TILE), BF),
            vm((7, 2, BLOCKS, 16, TILE), BF),
            vm((ROWS, 2, BLOCKS, 16, TILE), BF),
            vm((4, TILE, WIDTH), BF),
            vm(square, F32),
            vm(square, F32), vm(square, F32), vm(square, BF), vm(square, BF), vm(square, BF), vm(square, BF),
            vm((2, WIDTH, WIDTH), BF),
            vm((TILE, WIDTH), F32),
            [vm((n, 1, 256), F32) for n in (16, 16)],
            *sems,
            dma((4,)),
        ],
        compiler_params=pltpu.CompilerParams(
            collective_id=0, has_side_effects=True, vmem_limit_bytes=60 * 1024 * 1024
        ),
    )(owners, grad, stat_state)
    hbm = pl.BlockSpec(memory_space=pltpu.HBM)
    return pl.pallas_call(
        hand_over,
        out_shape=tuple(jax.ShapeDtypeStruct(a.shape, a.dtype) for a in results),
        in_specs=[hbm, hbm],
        out_specs=(hbm, hbm),
        scratch_shapes=[vm((2, WIDTH, WIDTH), F32), vm((TILE, WIDTH), BF), dma((2, 9))],
        compiler_params=pltpu.CompilerParams(vmem_limit_bytes=60 * 1024 * 1024),
    )(*results)


def hand_over(update, new, update_out, new_out, held, held_update, sems):
    ways = [(update, held_update, update_out)]
    for s in range(8):
        rows = pl.ds(s % 4 * TILE, TILE)
        ways.append((new.at[s // 4, rows], held.at[s // 4, rows], new_out.at[s // 4, rows]))
    into = [pltpu.make_async_copy(a, b, sems.at[0, s]) for s, (a, b, _) in enumerate(ways)]
    out = [pltpu.make_async_copy(b, c, sems.at[1, s]) for s, (_, b, c) in enumerate(ways)]
    for copy in into:
        copy.start()
    for copy, then in zip(into, out):
        copy.wait()
        then.start()
    for copy in out:
        copy.wait()


def solution(mesh):
    return jax.shard_map(
        shards,
        mesh=mesh,
        in_specs=(P("dp", "mp"), P("dp", "mp", None), P("mp", None)),
        out_specs=(P("dp", "mp"), P("dp", "mp", None)),
        check_vma=False,
    )
```

```python
import jax
import jax.numpy as jnp
from jax import lax
from jax.experimental import pallas as pl
from jax.experimental.pallas import tpu as pltpu
from jax.sharding import PartitionSpec as P

ITERS = 6
BETA = 0.9
EPS = 1e-06
MESH = pl.DeviceIdType.MESH
BF = jnp.bfloat16
F32 = jnp.float32

WIDTH = 512
TILE = 128
COUNT = 16
ROWS = 8
PAIRS = [(i, j) for i in range(4) for j in range(i + 1, 4)]
SIZES = (3, 2, 2, 2)
PARTS = len(SIZES)
SPOT = [(p, n) for p, size in enumerate(SIZES) for n in range(size)]
BACK_SIZES = (5, 4)
BACKS = len(BACK_SIZES)
BACK_SPOT = [(p, n) for p, size in enumerate(BACK_SIZES) for n in range(size)]


def block(ref, i, j):
    return ref[i * TILE:(i + 1) * TILE, j * TILE:(j + 1) * TILE]


def packed(ref):
    half = TILE // 2
    diag = [block(ref, d, d) for d in range(4)]
    upper = [jnp.concatenate([diag[d][:half], diag[d + 1][:half]], axis=0) for d in (0, 2)]
    left = lax.broadcasted_iota(jnp.int32, (half, TILE), 1) < half
    lower = [jnp.where(left, pltpu.roll(diag[d + 1][half:], half, 1), diag[d][half:]) for d in (0, 2)]
    blocks = upper + [jnp.concatenate(lower, axis=0)] + [block(ref, i, j) for i, j in PAIRS]
    return [b.astype(BF).reshape(ROWS, 16, TILE) for b in blocks]


def unpacked(get):
    half = TILE // 2
    low = lax.broadcasted_iota(jnp.int32, (TILE, TILE), 0) >= half
    left = lax.broadcasted_iota(jnp.int32, (TILE, TILE), 1) < half
    corners = get(2)
    for d in range(4):
        upper = get(d // 2)[d % 2 * half:(d % 2 + 1) * half]
        corner = corners[d // 2 * half:(d // 2 + 1) * half]
        if d % 2:
            corner = pltpu.roll(corner, half, 1)
        whole = jnp.concatenate([upper, corner], axis=0)
        yield d, d, jnp.where(low & left, whole.T, whole)
    for n, (i, j) in enumerate(PAIRS):
        yield i, j, get(3 + n)


def kernel(
    owners_hbm, grad, state_hbm, update, new_hbm,
    state, owners, positions, inverse,
    packs, spreads, crosses, relays, landeds, chosens, factors, stat_packs, stat_alls,
    stat_picks, stat_backs, gfull, stat,
    m_ref, x_ref, b_ref, p_ref, f_ref, xl_ref, roots, raw_ref, sums_a, sums_b,
    s1s, s1r, s2s, s2r, s3s, s3r, gs, gr, r1s, r1r, r2s, r2r, r3s, r3r, rts, rtr, pas, par, pbs, pbr, loc,
):
    me = lax.axis_index("dp")
    mp = lax.axis_index("mp")
    row, r = lax.div(me, 8), lax.rem(me, 8)
    x, c = lax.div(r, 2), lax.rem(r, 2)
    zlo, y = lax.div(mp, 4), lax.rem(mp, 4)
    quad = lax.rem(x, 2) * 2 + c

    def send(src, dst, ssem, rsem, dp, mp_to=None):
        copy = pltpu.make_async_remote_copy(
            src_ref=src, dst_ref=dst, send_sem=ssem, recv_sem=rsem,
            device_id=(dp, mp if mp_to is None else mp_to), device_id_type=MESH,
        )
        copy.start()
        return copy

    def sent(groups):
        for copies in groups:
            for copy in copies:
                copy.wait_send()

    def row_peer(t):
        return lax.rem(r + t, 8)

    def plane_peer(dx, dy):
        to_x, to_y = lax.rem(x + dx, 4), lax.rem(y + dy, 4)
        return row * 8 + to_x * 2 + c, zlo * 4 + to_y

    def column_peer(dh, dl, dc):
        to_row, to_lo, to_c = lax.rem(row + dh, 4), lax.rem(zlo + dl, 2), lax.rem(c + dc, 2)
        return to_row * 8 + x * 2 + to_c, to_lo * 4 + y

    plane = [(dx, dy) for dx in range(4) for dy in range(4) if dx or dy]
    column = [(dh, dl, dc) for dh in range(4) for dl in range(2) for dc in range(2) if dh or dl or dc]

    loads = [pltpu.make_async_copy(state_hbm.at[k], state.at[k], loc.at[k]) for k in range(2)]
    for load in loads:
        load.start()
    own_grad = pltpu.make_async_copy(grad, gfull.at[quad], loc.at[2])
    own_grad.start()
    own_table = pltpu.make_async_copy(owners_hbm, owners, loc.at[3])
    own_table.start()
    barrier = pltpu.get_barrier_semaphore()
    greeted = [(row * 8 + row_peer(t), mp) for t in range(1, ROWS)]
    greeted += [plane_peer(dx, dy) for dx, dy in plane if dy]
    greeted += [column_peer(*d) for d in column if d[0] or d[1]]
    for peer in greeted:
        pl.semaphore_signal(barrier, inc=1, device_id=peer, device_id_type=MESH)

    for k in range(2):
        loads[k].wait()
        for (part, at), piece in zip(SPOT, packed(state.at[k])):
            packs[part][:, k, at] = piece
    for part in range(PARTS):
        spreads[part][pl.ds(2 * r, 2)] = packs[part][r]
    pl.semaphore_wait(barrier, len(greeted))

    stage1 = []
    for part in range(PARTS):
        copies = []
        for t in range(1, ROWS):
            peer = row_peer(t)
            s = part * 7 + t - 1
            copies.append(send(packs[part].at[peer], spreads[part].at[pl.ds(2 * r, 2)], s1s.at[s], s1r.at[s], row * 8 + peer))
        stage1.append(copies)
    own_grad.wait()
    other = x + 1 - 2 * lax.rem(x, 2)
    sibling = row * 8 + x * 2 + 1 - c
    own_rows = gfull.at[quad]
    g_copies = [
        send(own_rows, own_rows, gs.at[0], gr.at[0], row * 8 + other * 2 + c),
        send(own_rows, own_rows, gs.at[1], gr.at[1], sibling),
    ]

    own_table.wait()
    table = [owners[0, f] for f in range(COUNT)]
    place = []
    for f in range(COUNT):
        slot = jnp.int32(0)
        for g in range(f):
            slot = slot + jnp.where(table[g] == table[f], 1, 0)
        place.append(table[f] * 2 + slot)
        positions[f] = place[f]

    def invert(index, carry):
        target = row * 16 + index
        found = jnp.int32(-1)
        for f in range(COUNT):
            found = jnp.where(positions[f] == target, f, found)
        inverse[index] = found
        return carry

    lax.fori_loop(0, COUNT, invert, 0)

    wide = gfull[quad].astype(F32)
    grad_sum = jnp.sum(wide * wide, axis=0, keepdims=True)
    grad_sum = grad_sum[:, :128] + grad_sum[:, 128:256] + grad_sum[:, 256:384] + grad_sum[:, 384:]

    def turned(by):
        return lax.rem(row + by, 4)

    ways = (1, 3) * (PARTS // 2)
    back_ways = (1, 3)
    stage2 = []

    def cross(part):
        way = ways[part]
        for copy in stage1[part]:
            copy.wait_recv()

        def own(to_row, q):
            return spreads[part][jnp.clip(positions[to_row * 4 + q] - row * 16, 0, 15)]

        s = part * 3
        copies = []
        for q in range(4):
            crosses[part][0, q] = own(turned(2), q)
        copies.append(send(crosses[part].at[0], relays[part], s2s.at[s], s2r.at[s], turned(way) * 8 + r))
        for q in range(4):
            crosses[part][1, q] = own(turned(4 - way), q)
        copies.append(send(crosses[part].at[1], landeds[part].at[pl.ds(8, 4)], s2s.at[s + 1], s2r.at[s + 1], turned(4 - way) * 8 + r))
        for q in range(4):
            landeds[part][q] = own(row, q)
        stage2.append(copies)

    def merge(part):
        way = ways[part]
        stage2[part][0].wait_recv()
        s = part * 3
        for q in range(4):
            place_q = positions[turned(way) * 4 + q] - row * 16
            is_own = (place_q >= 0) & (place_q < 16)
            crosses[part][2, q] = jnp.where(is_own, spreads[part][jnp.clip(place_q, 0, 15)], relays[part][q])
        stage2[part].append(send(crosses[part].at[2], landeds[part].at[pl.ds(4, 4)], s2s.at[s + 2], s2r.at[s + 2], turned(way) * 8 + r))

    cross(0)
    cross(1)
    cross(2)
    merge(0)
    cross(3)
    merge(1)
    g_copies[0].wait_recv()
    other_rows = gfull.at[lax.rem(other, 2) * 2 + c]
    g_copies.append(send(other_rows, other_rows, gs.at[2], gr.at[2], sibling))
    merge(2)
    merge(3)

    g_copies[1].wait_recv()
    g_copies[2].wait_recv()
    g = gfull[...].reshape(WIDTH, WIDTH)

    @pl.when(c == 0)
    def _():
        stat[...] = lax.dot_general(g, g, (((1,), (1,)), ((), ())), preferred_element_type=F32)

    @pl.when(c == 1)
    def _():
        stat[...] = lax.dot_general(g.T, g, (((1,), (0,)), ((), ())), preferred_element_type=F32)

    mine = row * 4 + lax.div(x, 2) * 2 + c
    outer = lax.rem(x + 3 + 2 * lax.rem(x, 2), 4)
    back1 = []
    for (part, at), piece in zip(BACK_SPOT, packed(stat)):
        stat_packs[part][:, at] = piece
    for part in range(BACKS):
        stat_alls[part][mine] = stat_packs[part][r]
        copies = []
        for s, (to_x, to_c) in enumerate([(x, 1 - c), (outer, c), (outer, 1 - c)]):
            to, s = to_x * 2 + to_c, s + part * 3
            copies.append(send(stat_packs[part].at[to], stat_alls[part].at[mine], r1s.at[s], r1r.at[s], row * 8 + to))
        back1.append(copies)

    stage3 = []
    back2 = []
    for part in range(PARTS):
        stage2[part][1].wait_recv()
        stage2[part][2].wait_recv()
        for q in range(4):
            origin = lax.div(positions[row * 4 + q], 16)
            t = lax.rem(row - origin + 4, 4) if ways[part] == 1 else lax.rem(origin - row + 4, 4)
            chosens[part][q] = landeds[part][jnp.where(t >= 2, t - 1, t) * 4 + q]
        copies = []
        for t in range(1, ROWS):
            peer = row_peer(t)
            q = lax.div(peer, 4) * 2 + lax.rem(peer, 2)
            s = part * 7 + t - 1
            copies.append(send(chosens[part].at[q], factors[part].at[r], s3s.at[s], s3r.at[s], row * 8 + peer))
        factors[part][r] = chosens[part][lax.div(x, 2) * 2 + c]
        stage3.append(copies)

        if part == 0:
            for back, way in enumerate(back_ways):
                for copy in back1[back]:
                    copy.wait_recv()
                here = stat_alls[back].at[pl.ds(4 * row, 4)]
                s = back * 3
                copies = []
                for t, by in enumerate((way, 4 - way)):
                    copies.append(send(here, here, r2s.at[s + t], r2r.at[s + t], turned(by) * 8 + r))
                back2.append(copies)

    sent(stage1 + stage2 + back1 + [g_copies])

    norm = jnp.zeros((TILE, TILE), F32)
    def arrived(n):
        part, at = SPOT[n]
        if part not in here:
            here.append(part)
            for copy in stage3[part]:
                copy.wait_recv()
        return factors[part][:, at].reshape(TILE, TILE).astype(F32)

    here = []
    for i, j, old in unpacked(arrived):
        mixed = BETA * old + (1.0 - BETA) * block(stat, i, j)
        m_ref[i * TILE:(i + 1) * TILE, j * TILE:(j + 1) * TILE] = mixed
        if i == j:
            norm = norm + mixed * mixed
        else:
            m_ref[j * TILE:(j + 1) * TILE, i * TILE:(i + 1) * TILE] = mixed.T
            norm = norm + 2.0 * (mixed * mixed)
    total = jnp.sum(jnp.sum(norm, axis=0, keepdims=True), axis=1, keepdims=True)
    scale = jnp.sqrt(total + EPS)
    inverse_scale = 1.0 / scale
    start = lax.rsqrt(jnp.sqrt(scale))

    further = []
    for part, way in enumerate(back_ways):
        here = stat_alls[part].at[pl.ds(4 * turned(4 - way), 4)]
        s = part * 3 + 2
        further.append(pltpu.make_async_remote_copy(
            src_ref=here, dst_ref=here, send_sem=r2s.at[s], recv_sem=r2r.at[s],
            device_id=(turned(way) * 8 + r, mp), device_id_type=MESH,
        ))

    HALF = WIDTH // 2
    halves = [pl.ds(h * HALF, HALF) for h in range(2)]
    for h, rows in enumerate(halves):
        reduced = m_ref[rows] * inverse_scale
        m_ref[rows] = reduced
        b_ref[rows] = reduced.astype(BF)
        at = lax.broadcasted_iota(jnp.int32, (HALF, WIDTH), 0) + h * HALF
        eye = at == lax.broadcasted_iota(jnp.int32, (HALF, WIDTH), 1)
        x_ref[rows] = jnp.where(eye, start, 0.0)

    def dot(a, b):
        return jnp.dot(a, b, preferred_element_type=F32)

    def apply(cols):
        return 1.25 * x_ref[:, cols] - 0.25 * dot(xl_ref[...], b_ref[:, cols])

    def step(index, carry):
        @pl.when(index == 1)
        def _():
            for part in range(BACKS):
                back2[part][0].wait_recv()
                further[part].start()

        xl_ref[...] = x_ref[...].astype(BF)
        for cols in halves:
            p_ref[:, cols] = (dot(b_ref[...], b_ref[:, cols]) * 0.0625 - 0.625 * b_ref[:, cols].astype(F32)).astype(BF)
        x_ref[:, halves[0]] = apply(halves[0])
        for cols in halves:
            f_ref[:, cols] = (dot(p_ref[...], p_ref[:, cols]) + 3.125 * p_ref[:, cols].astype(F32)).astype(BF)
        x_ref[:, halves[1]] = apply(halves[1])
        for cols in halves:
            after = 2.44140625 * m_ref[:, cols] + dot(f_ref[...], b_ref[:, cols])
            m_ref[:, cols] = after
            b_ref[:, cols] = after.astype(BF)
        return carry

    lax.fori_loop(0, ITERS - 1, step, 0)
    for part in range(BACKS):
        back2[part].append(further[part])

    for copies in back2:
        copies[1].wait_recv()
        copies[2].wait_recv()
    back3 = []
    for part in range(BACKS):
        for t in range(1, ROWS):
            peer = row_peer(t)
            for k in range(2):
                stat_picks[part][t - 1, k] = stat_alls[part][jnp.maximum(inverse[2 * peer + k], 0)]
            s = part * 7 + t - 1
            back3.append(send(stat_picks[part].at[t - 1], stat_backs[part].at[r], r3s.at[s], r3r.at[s], row * 8 + peer))
        for k in range(2):
            stat_backs[part][r, k] = stat_alls[part][jnp.maximum(inverse[2 * r + k], 0)]

    root_copies = []
    xl_ref[...] = x_ref[...].astype(BF)
    for h, cols in enumerate(halves):
        roots[c, :, cols] = apply(cols).astype(BF)
        here = roots.at[c, :, cols]
        root_copies.append(send(here, here, rts.at[h], rtr.at[h], sibling))

    for copy in root_copies:
        copy.wait_recv()
    left = roots[0, pl.ds(quad * TILE, TILE)]
    first = dot(left, gfull[...].reshape(WIDTH, WIDTH)).astype(BF)
    raw = dot(first, roots[1])
    raw_ref[...] = raw
    raw_sum = jnp.sum(raw * raw, axis=0, keepdims=True)
    raw_sum = raw_sum[:, :128] + raw_sum[:, 128:256] + raw_sum[:, 256:384] + raw_sum[:, 384:]

    v = row * 4 + zlo * 2 + c
    sums_a[v, :, :128] = grad_sum
    sums_a[v, :, 128:] = raw_sum
    round_a = []
    for s, d in enumerate(column):
        dp, to_mp = column_peer(*d)
        round_a.append(send(sums_a.at[v], sums_a.at[v], pas.at[s], par.at[s], dp, to_mp))
    sent(stage3 + back2 + [root_copies])
    for copy in round_a:
        copy.wait_recv()
    u = x * 4 + y
    sums_b[u] = jnp.sum(sums_a[...], axis=0)
    round_b = []
    for s, d in enumerate(plane):
        dp, to_mp = plane_peer(*d)
        round_b.append(send(sums_b.at[u], sums_b.at[u], pbs.at[s], pbr.at[s], dp, to_mp))


    for copy in back3:
        copy.wait_recv()
    stores = []
    for k in range(2):
        present = inverse[2 * r + k] >= 0

        def returned(n):
            part, at = BACK_SPOT[n]
            return stat_backs[part][:, k, at].reshape(TILE, TILE).astype(F32)

        for i, j, got in unpacked(returned):
            for a, b, value in ((i, j, got),) + (((j, i, got.T),) if i != j else ()):
                old = state[k, a * TILE:(a + 1) * TILE, b * TILE:(b + 1) * TILE]
                state[k, a * TILE:(a + 1) * TILE, b * TILE:(b + 1) * TILE] = jnp.where(
                    present, BETA * old + (1.0 - BETA) * value, old
                )
        store = pltpu.make_async_copy(state.at[k], new_hbm.at[k], loc.at[k])
        store.start()
        stores.append(store)

    sent([round_a, back3, round_b])
    for copy in round_b:
        copy.wait_recv()
    both = jnp.sum(sums_b[...], axis=0)
    grad_total = jnp.sum(both[:, :128], axis=1, keepdims=True)
    raw_total = jnp.sum(both[:, 128:], axis=1, keepdims=True)
    ratio = jnp.sqrt(grad_total / (raw_total + EPS))
    update[...] = (raw_ref[...] * ratio).astype(BF)

    for store in stores:
        store.wait()


def shards(grad, stat_state, owners):
    dma = pltpu.SemaphoreType.DMA
    vm = pltpu.VMEM

    def parted(*shape):
        return [vm(shape + (size, 16, TILE), BF) for size in SIZES]

    def backed(*shape):
        return [vm(shape + (size, 16, TILE), BF) for size in BACK_SIZES]

    sems = []
    for count in (7 * PARTS, 3 * PARTS, 7 * PARTS, 3, 3 * BACKS, 3 * BACKS, 7 * BACKS, 2, 15, 15):
        sems += [dma((count,)), dma((count,))]
    square = (WIDTH, WIDTH)
    results = pl.pallas_call(
        kernel,
        out_shape=(
            jax.ShapeDtypeStruct((TILE, WIDTH), BF),
            jax.ShapeDtypeStruct((2, WIDTH, WIDTH), F32),
        ),
        in_specs=[
            pl.BlockSpec(memory_space=pltpu.HBM),
            pl.BlockSpec(memory_space=pltpu.HBM),
            pl.BlockSpec(memory_space=pltpu.HBM),
        ],
        out_specs=(pl.BlockSpec(memory_space=pltpu.VMEM), pl.BlockSpec(memory_space=pl.ANY)),
        scratch_shapes=[
            vm((2, WIDTH, WIDTH), F32),
            pltpu.SMEM((1, COUNT), jnp.int32),
            pltpu.SMEM((COUNT,), jnp.int32),
            pltpu.SMEM((COUNT,), jnp.int32),
            parted(ROWS, 2), parted(16), parted(3, 4), parted(4), parted(12), parted(4), parted(ROWS),
            backed(ROWS), backed(COUNT), backed(7, 2), backed(ROWS, 2),
            vm((4, TILE, WIDTH), BF),
            vm(square, F32),
            vm(square, F32), vm(square, F32), vm(square, BF), vm(square, BF), vm(square, BF), vm(square, BF),
            vm((2, WIDTH, WIDTH), BF),
            vm((TILE, WIDTH), F32),
            vm((16, 1, 256), F32),
            vm((16, 1, 256), F32),
            *sems,
            dma((4,)),
        ],
        compiler_params=pltpu.CompilerParams(
            collective_id=0, has_side_effects=True, vmem_limit_bytes=60 * 1024 * 1024
        ),
    )(owners, grad, stat_state)
    hbm = pl.BlockSpec(memory_space=pltpu.HBM)
    return pl.pallas_call(
        hand_over,
        out_shape=tuple(jax.ShapeDtypeStruct(a.shape, a.dtype) for a in results),
        in_specs=[hbm, hbm],
        out_specs=(hbm, hbm),
        scratch_shapes=[vm((2, WIDTH, WIDTH), F32), vm((TILE, WIDTH), BF), dma((2, 9))],
        compiler_params=pltpu.CompilerParams(vmem_limit_bytes=60 * 1024 * 1024),
    )(*results)


def hand_over(update, new, update_out, new_out, held, held_update, sems):
    ways = [(update, held_update, update_out)]
    for s in range(8):
        rows = pl.ds(s % 4 * TILE, TILE)
        ways.append((new.at[s // 4, rows], held.at[s // 4, rows], new_out.at[s // 4, rows]))
    into = [pltpu.make_async_copy(a, b, sems.at[0, s]) for s, (a, b, _) in enumerate(ways)]
    out = [pltpu.make_async_copy(b, c, sems.at[1, s]) for s, (_, b, c) in enumerate(ways)]
    for copy in into:
        copy.start()
    for copy, then in zip(into, out):
        copy.wait()
        then.start()
    for copy in out:
        copy.wait()


def solution(mesh):
    return jax.shard_map(
        shards,
        mesh=mesh,
        in_specs=(P("dp", "mp"), P("dp", "mp", None), P("mp", None)),
        out_specs=(P("dp", "mp"), P("dp", "mp", None)),
        check_vma=False,
    )
```

```python
import jax
import jax.numpy as jnp
from jax import lax
from jax.experimental import pallas as pl
from jax.experimental.pallas import tpu as pltpu
from jax.sharding import PartitionSpec as P

ITERS = 6
BETA = 0.9
EPS = 1e-06
MESH = pl.DeviceIdType.MESH
BF = jnp.bfloat16
F32 = jnp.float32

WIDTH = 512
TILE = 128
COUNT = 16
ROWS = 8
PAIRS = [(i, j) for i in range(4) for j in range(i + 1, 4)]
SIZES = (5, 4)
PARTS = len(SIZES)
SPOT = [(p, n) for p, size in enumerate(SIZES) for n in range(size)]
BACK_SIZES = (5, 4)
BACKS = len(BACK_SIZES)
BACK_SPOT = [(p, n) for p, size in enumerate(BACK_SIZES) for n in range(size)]


def block(ref, i, j):
    return ref[i * TILE:(i + 1) * TILE, j * TILE:(j + 1) * TILE]


def packed(ref):
    half = TILE // 2
    diag = [block(ref, d, d) for d in range(4)]
    upper = [jnp.concatenate([diag[d][:half], diag[d + 1][:half]], axis=0) for d in (0, 2)]
    left = lax.broadcasted_iota(jnp.int32, (half, TILE), 1) < half
    lower = [jnp.where(left, pltpu.roll(diag[d + 1][half:], half, 1), diag[d][half:]) for d in (0, 2)]
    blocks = upper + [jnp.concatenate(lower, axis=0)] + [block(ref, i, j) for i, j in PAIRS]
    return [b.astype(BF).reshape(ROWS, 16, TILE) for b in blocks]


def unpacked(get):
    half = TILE // 2
    low = lax.broadcasted_iota(jnp.int32, (TILE, TILE), 0) >= half
    left = lax.broadcasted_iota(jnp.int32, (TILE, TILE), 1) < half
    corners = get(2)
    for d in range(4):
        upper = get(d // 2)[d % 2 * half:(d % 2 + 1) * half]
        corner = corners[d // 2 * half:(d // 2 + 1) * half]
        if d % 2:
            corner = pltpu.roll(corner, half, 1)
        whole = jnp.concatenate([upper, corner], axis=0)
        yield d, d, jnp.where(low & left, whole.T, whole)
    for n, (i, j) in enumerate(PAIRS):
        yield i, j, get(3 + n)


def kernel(
    owners_hbm, grad, state_hbm, update, new_hbm,
    state, owners, positions, inverse,
    packs, spreads, crosses, relays, landeds, chosens, factors, stat_packs, stat_alls,
    stat_picks, stat_backs, gfull, stat,
    m_ref, x_ref, b_ref, p_ref, f_ref, xl_ref, roots, raw_ref, sums_a, sums_b,
    s1s, s1r, s2s, s2r, s3s, s3r, gs, gr, r1s, r1r, r2s, r2r, r3s, r3r, rts, rtr, pas, par, pbs, pbr, loc,
):
    me = lax.axis_index("dp")
    mp = lax.axis_index("mp")
    row, r = lax.div(me, 8), lax.rem(me, 8)
    x, c = lax.div(r, 2), lax.rem(r, 2)
    zlo, y = lax.div(mp, 4), lax.rem(mp, 4)
    quad = lax.rem(x, 2) * 2 + c

    def send(src, dst, ssem, rsem, dp, mp_to=None):
        copy = pltpu.make_async_remote_copy(
            src_ref=src, dst_ref=dst, send_sem=ssem, recv_sem=rsem,
            device_id=(dp, mp if mp_to is None else mp_to), device_id_type=MESH,
        )
        copy.start()
        return copy

    def sent(groups):
        for copies in groups:
            for copy in copies:
                copy.wait_send()

    def row_peer(t):
        return lax.rem(r + t, 8)

    def plane_peer(dx, dy):
        to_x, to_y = lax.rem(x + dx, 4), lax.rem(y + dy, 4)
        return row * 8 + to_x * 2 + c, zlo * 4 + to_y

    def column_peer(dh, dl, dc):
        to_row, to_lo, to_c = lax.rem(row + dh, 4), lax.rem(zlo + dl, 2), lax.rem(c + dc, 2)
        return to_row * 8 + x * 2 + to_c, to_lo * 4 + y

    plane = [(dx, dy) for dx in range(4) for dy in range(4) if dx or dy]
    column = [(dh, dl, dc) for dh in range(4) for dl in range(2) for dc in range(2) if dh or dl or dc]

    loads = [pltpu.make_async_copy(state_hbm.at[k], state.at[k], loc.at[k]) for k in range(2)]
    for load in loads:
        load.start()
    own_grad = pltpu.make_async_copy(grad, gfull.at[quad], loc.at[2])
    own_grad.start()
    own_table = pltpu.make_async_copy(owners_hbm, owners, loc.at[3])
    own_table.start()
    barrier = pltpu.get_barrier_semaphore()
    greeted = [(row * 8 + row_peer(t), mp) for t in range(1, ROWS)]
    greeted += [plane_peer(dx, dy) for dx, dy in plane if dy]
    greeted += [column_peer(*d) for d in column if d[0] or d[1]]
    for peer in greeted:
        pl.semaphore_signal(barrier, inc=1, device_id=peer, device_id_type=MESH)

    for k in range(2):
        loads[k].wait()
        for (part, at), piece in zip(SPOT, packed(state.at[k])):
            packs[part][:, k, at] = piece
    for part in range(PARTS):
        spreads[part][pl.ds(2 * r, 2)] = packs[part][r]
    pl.semaphore_wait(barrier, len(greeted))

    own_grad.wait()
    other = x + 1 - 2 * lax.rem(x, 2)
    sibling = row * 8 + x * 2 + 1 - c
    own_rows = gfull.at[quad]

    stage1 = []
    for part in range(PARTS):
        copies = []
        for t in range(1, ROWS):
            peer = row_peer(t)
            s = part * 7 + t - 1
            copies.append(send(packs[part].at[peer], spreads[part].at[pl.ds(2 * r, 2)], s1s.at[s], s1r.at[s], row * 8 + peer))
        stage1.append(copies)
        if part == 0:
            g_copies = [
                send(own_rows, own_rows, gs.at[0], gr.at[0], row * 8 + other * 2 + c),
                send(own_rows, own_rows, gs.at[1], gr.at[1], sibling),
            ]

    own_table.wait()
    table = [owners[0, f] for f in range(COUNT)]
    place = []
    for f in range(COUNT):
        slot = jnp.int32(0)
        for g in range(f):
            slot = slot + jnp.where(table[g] == table[f], 1, 0)
        place.append(table[f] * 2 + slot)
        positions[f] = place[f]

    def invert(index, carry):
        target = row * 16 + index
        found = jnp.int32(-1)
        for f in range(COUNT):
            found = jnp.where(positions[f] == target, f, found)
        inverse[index] = found
        return carry

    lax.fori_loop(0, COUNT, invert, 0)

    wide = gfull[quad].astype(F32)
    grad_sum = jnp.sum(wide * wide, axis=0, keepdims=True)
    grad_sum = grad_sum[:, :128] + grad_sum[:, 128:256] + grad_sum[:, 256:384] + grad_sum[:, 384:]

    def turned(by):
        return lax.rem(row + by, 4)

    ways = (1, 3) * (PARTS // 2)
    back_ways = (1, 3)
    stage2 = []

    def cross(part):
        way = ways[part]
        for copy in stage1[part]:
            copy.wait_recv()

        def own(to_row, q):
            return spreads[part][jnp.clip(positions[to_row * 4 + q] - row * 16, 0, 15)]

        s = part * 3
        copies = []
        for q in range(4):
            crosses[part][0, q] = own(turned(2), q)
        copies.append(send(crosses[part].at[0], relays[part], s2s.at[s], s2r.at[s], turned(way) * 8 + r))
        for q in range(4):
            crosses[part][1, q] = own(turned(4 - way), q)
        copies.append(send(crosses[part].at[1], landeds[part].at[pl.ds(8, 4)], s2s.at[s + 1], s2r.at[s + 1], turned(4 - way) * 8 + r))
        for q in range(4):
            landeds[part][q] = own(row, q)
        stage2.append(copies)

    def merge(part):
        way = ways[part]
        stage2[part][0].wait_recv()
        s = part * 3
        for q in range(4):
            place_q = positions[turned(way) * 4 + q] - row * 16
            is_own = (place_q >= 0) & (place_q < 16)
            crosses[part][2, q] = jnp.where(is_own, spreads[part][jnp.clip(place_q, 0, 15)], relays[part][q])
        stage2[part].append(send(crosses[part].at[2], landeds[part].at[pl.ds(4, 4)], s2s.at[s + 2], s2r.at[s + 2], turned(way) * 8 + r))

    cross(0)
    cross(1)
    g_copies[0].wait_recv()
    other_rows = gfull.at[lax.rem(other, 2) * 2 + c]
    g_copies.append(send(other_rows, other_rows, gs.at[2], gr.at[2], sibling))
    merge(0)
    merge(1)

    g_copies[1].wait_recv()
    g_copies[2].wait_recv()
    g = gfull[...].reshape(WIDTH, WIDTH)

    @pl.when(c == 0)
    def _():
        stat[...] = lax.dot_general(g, g, (((1,), (1,)), ((), ())), preferred_element_type=F32)

    @pl.when(c == 1)
    def _():
        stat[...] = lax.dot_general(g.T, g, (((1,), (0,)), ((), ())), preferred_element_type=F32)

    mine = row * 4 + lax.div(x, 2) * 2 + c
    outer = lax.rem(x + 3 + 2 * lax.rem(x, 2), 4)
    back1 = []
    for (part, at), piece in zip(BACK_SPOT, packed(stat)):
        stat_packs[part][:, at] = piece
    for part in range(BACKS):
        stat_alls[part][mine] = stat_packs[part][r]
        copies = []
        for s, (to_x, to_c) in enumerate([(x, 1 - c), (outer, c), (outer, 1 - c)]):
            to, s = to_x * 2 + to_c, s + part * 3
            copies.append(send(stat_packs[part].at[to], stat_alls[part].at[mine], r1s.at[s], r1r.at[s], row * 8 + to))
        back1.append(copies)

    stage3 = []
    back2 = []
    for part in range(PARTS):
        stage2[part][1].wait_recv()
        stage2[part][2].wait_recv()
        for q in range(4):
            origin = lax.div(positions[row * 4 + q], 16)
            t = lax.rem(row - origin + 4, 4) if ways[part] == 1 else lax.rem(origin - row + 4, 4)
            chosens[part][q] = landeds[part][jnp.where(t >= 2, t - 1, t) * 4 + q]
        copies = []
        for t in range(1, ROWS):
            peer = row_peer(t)
            q = lax.div(peer, 4) * 2 + lax.rem(peer, 2)
            s = part * 7 + t - 1
            copies.append(send(chosens[part].at[q], factors[part].at[r], s3s.at[s], s3r.at[s], row * 8 + peer))
        factors[part][r] = chosens[part][lax.div(x, 2) * 2 + c]
        stage3.append(copies)

        if part == 0:
            for back, way in enumerate(back_ways):
                for copy in back1[back]:
                    copy.wait_recv()
                here = stat_alls[back].at[pl.ds(4 * row, 4)]
                s = back * 3
                copies = []
                for t, by in enumerate((way, 4 - way)):
                    copies.append(send(here, here, r2s.at[s + t], r2r.at[s + t], turned(by) * 8 + r))
                back2.append(copies)

    sent(stage1 + stage2 + back1 + [g_copies])

    norm = jnp.zeros((TILE, TILE), F32)
    def arrived(n):
        part, at = SPOT[n]
        if part not in here:
            here.append(part)
            for copy in stage3[part]:
                copy.wait_recv()
        return factors[part][:, at].reshape(TILE, TILE).astype(F32)

    here = []
    for i, j, old in unpacked(arrived):
        mixed = BETA * old + (1.0 - BETA) * block(stat, i, j)
        m_ref[i * TILE:(i + 1) * TILE, j * TILE:(j + 1) * TILE] = mixed
        if i == j:
            norm = norm + mixed * mixed
        else:
            m_ref[j * TILE:(j + 1) * TILE, i * TILE:(i + 1) * TILE] = mixed.T
            norm = norm + 2.0 * (mixed * mixed)
    total = jnp.sum(jnp.sum(norm, axis=0, keepdims=True), axis=1, keepdims=True)
    scale = jnp.sqrt(total + EPS)
    inverse_scale = 1.0 / scale
    start = lax.rsqrt(jnp.sqrt(scale))

    further = []
    for part, way in enumerate(back_ways):
        here = stat_alls[part].at[pl.ds(4 * turned(4 - way), 4)]
        s = part * 3 + 2
        further.append(pltpu.make_async_remote_copy(
            src_ref=here, dst_ref=here, send_sem=r2s.at[s], recv_sem=r2r.at[s],
            device_id=(turned(way) * 8 + r, mp), device_id_type=MESH,
        ))

    HALF = WIDTH // 2
    halves = [pl.ds(h * HALF, HALF) for h in range(2)]
    for h, rows in enumerate(halves):
        reduced = m_ref[rows] * inverse_scale
        m_ref[rows] = reduced
        b_ref[rows] = reduced.astype(BF)
        at = lax.broadcasted_iota(jnp.int32, (HALF, WIDTH), 0) + h * HALF
        eye = at == lax.broadcasted_iota(jnp.int32, (HALF, WIDTH), 1)
        x_ref[rows] = jnp.where(eye, start, 0.0)

    def dot(a, b):
        return jnp.dot(a, b, preferred_element_type=F32)

    def apply(cols):
        return 1.25 * x_ref[:, cols] - 0.25 * dot(xl_ref[...], b_ref[:, cols])

    def step(index, carry):
        @pl.when(index == 2)
        def _():
            for part in range(BACKS):
                back2[part][0].wait_recv()
                further[part].start()

        xl_ref[...] = x_ref[...].astype(BF)
        for cols in halves:
            p_ref[:, cols] = (dot(b_ref[...], b_ref[:, cols]) * 0.0625 - 0.625 * b_ref[:, cols].astype(F32)).astype(BF)
        x_ref[:, halves[0]] = apply(halves[0])
        for cols in halves:
            f_ref[:, cols] = (dot(p_ref[...], p_ref[:, cols]) + 3.125 * p_ref[:, cols].astype(F32)).astype(BF)
        x_ref[:, halves[1]] = apply(halves[1])
        for cols in halves:
            after = 2.44140625 * m_ref[:, cols] + dot(f_ref[...], b_ref[:, cols])
            m_ref[:, cols] = after
            b_ref[:, cols] = after.astype(BF)
        return carry

    lax.fori_loop(0, ITERS - 1, step, 0)
    for part in range(BACKS):
        back2[part].append(further[part])

    for copies in back2:
        copies[1].wait_recv()
        copies[2].wait_recv()
    back3 = []
    for part in range(BACKS):
        for t in range(1, ROWS):
            peer = row_peer(t)
            for k in range(2):
                stat_picks[part][t - 1, k] = stat_alls[part][jnp.maximum(inverse[2 * peer + k], 0)]
            s = part * 7 + t - 1
            back3.append(send(stat_picks[part].at[t - 1], stat_backs[part].at[r], r3s.at[s], r3r.at[s], row * 8 + peer))
        for k in range(2):
            stat_backs[part][r, k] = stat_alls[part][jnp.maximum(inverse[2 * r + k], 0)]

    root_copies = []
    xl_ref[...] = x_ref[...].astype(BF)
    for h, cols in enumerate(halves):
        roots[c, :, cols] = apply(cols).astype(BF)
        here = roots.at[c, :, cols]
        root_copies.append(send(here, here, rts.at[h], rtr.at[h], sibling))

    for copy in root_copies:
        copy.wait_recv()
    left = roots[0, pl.ds(quad * TILE, TILE)]
    first = dot(left, gfull[...].reshape(WIDTH, WIDTH)).astype(BF)
    raw = dot(first, roots[1])
    raw_ref[...] = raw
    raw_sum = jnp.sum(raw * raw, axis=0, keepdims=True)
    raw_sum = raw_sum[:, :128] + raw_sum[:, 128:256] + raw_sum[:, 256:384] + raw_sum[:, 384:]

    v = row * 4 + zlo * 2 + c
    sums_a[v, :, :128] = grad_sum
    sums_a[v, :, 128:] = raw_sum
    round_a = []
    for s, d in enumerate(column):
        dp, to_mp = column_peer(*d)
        round_a.append(send(sums_a.at[v], sums_a.at[v], pas.at[s], par.at[s], dp, to_mp))
    sent(stage3 + back2 + [root_copies])
    for copy in round_a:
        copy.wait_recv()
    u = x * 4 + y
    sums_b[u] = jnp.sum(sums_a[...], axis=0)
    round_b = []
    for s, d in enumerate(plane):
        dp, to_mp = plane_peer(*d)
        round_b.append(send(sums_b.at[u], sums_b.at[u], pbs.at[s], pbr.at[s], dp, to_mp))


    for copy in back3:
        copy.wait_recv()
    stores = []
    for k in range(2):
        present = inverse[2 * r + k] >= 0

        def returned(n):
            part, at = BACK_SPOT[n]
            return stat_backs[part][:, k, at].reshape(TILE, TILE).astype(F32)

        for i, j, got in unpacked(returned):
            for a, b, value in ((i, j, got),) + (((j, i, got.T),) if i != j else ()):
                old = state[k, a * TILE:(a + 1) * TILE, b * TILE:(b + 1) * TILE]
                state[k, a * TILE:(a + 1) * TILE, b * TILE:(b + 1) * TILE] = jnp.where(
                    present, BETA * old + (1.0 - BETA) * value, old
                )
        store = pltpu.make_async_copy(state.at[k], new_hbm.at[k], loc.at[k])
        store.start()
        stores.append(store)

    sent([round_a, back3, round_b])
    for copy in round_b:
        copy.wait_recv()
    both = jnp.sum(sums_b[...], axis=0)
    grad_total = jnp.sum(both[:, :128], axis=1, keepdims=True)
    raw_total = jnp.sum(both[:, 128:], axis=1, keepdims=True)
    ratio = jnp.sqrt(grad_total / (raw_total + EPS))
    update[...] = (raw_ref[...] * ratio).astype(BF)

    for store in stores:
        store.wait()


def shards(grad, stat_state, owners):
    dma = pltpu.SemaphoreType.DMA
    vm = pltpu.VMEM

    def parted(*shape):
        return [vm(shape + (size, 16, TILE), BF) for size in SIZES]

    def backed(*shape):
        return [vm(shape + (size, 16, TILE), BF) for size in BACK_SIZES]

    sems = []
    for count in (7 * PARTS, 3 * PARTS, 7 * PARTS, 3, 3 * BACKS, 3 * BACKS, 7 * BACKS, 2, 15, 15):
        sems += [dma((count,)), dma((count,))]
    square = (WIDTH, WIDTH)
    results = pl.pallas_call(
        kernel,
        out_shape=(
            jax.ShapeDtypeStruct((TILE, WIDTH), BF),
            jax.ShapeDtypeStruct((2, WIDTH, WIDTH), F32),
        ),
        in_specs=[
            pl.BlockSpec(memory_space=pltpu.HBM),
            pl.BlockSpec(memory_space=pltpu.HBM),
            pl.BlockSpec(memory_space=pltpu.HBM),
        ],
        out_specs=(pl.BlockSpec(memory_space=pltpu.VMEM), pl.BlockSpec(memory_space=pl.ANY)),
        scratch_shapes=[
            vm((2, WIDTH, WIDTH), F32),
            pltpu.SMEM((1, COUNT), jnp.int32),
            pltpu.SMEM((COUNT,), jnp.int32),
            pltpu.SMEM((COUNT,), jnp.int32),
            parted(ROWS, 2), parted(16), parted(3, 4), parted(4), parted(12), parted(4), parted(ROWS),
            backed(ROWS), backed(COUNT), backed(7, 2), backed(ROWS, 2),
            vm((4, TILE, WIDTH), BF),
            vm(square, F32),
            vm(square, F32), vm(square, F32), vm(square, BF), vm(square, BF), vm(square, BF), vm(square, BF),
            vm((2, WIDTH, WIDTH), BF),
            vm((TILE, WIDTH), F32),
            vm((16, 1, 256), F32),
            vm((16, 1, 256), F32),
            *sems,
            dma((4,)),
        ],
        compiler_params=pltpu.CompilerParams(
            collective_id=0, has_side_effects=True, vmem_limit_bytes=60 * 1024 * 1024
        ),
    )(owners, grad, stat_state)
    hbm = pl.BlockSpec(memory_space=pltpu.HBM)
    return pl.pallas_call(
        hand_over,
        out_shape=tuple(jax.ShapeDtypeStruct(a.shape, a.dtype) for a in results),
        in_specs=[hbm, hbm],
        out_specs=(hbm, hbm),
        scratch_shapes=[vm((2, WIDTH, WIDTH), F32), vm((TILE, WIDTH), BF), dma((2, 9))],
        compiler_params=pltpu.CompilerParams(vmem_limit_bytes=60 * 1024 * 1024),
    )(*results)


def hand_over(update, new, update_out, new_out, held, held_update, sems):
    ways = [(update, held_update, update_out)]
    for s in range(8):
        rows = pl.ds(s % 4 * TILE, TILE)
        ways.append((new.at[s // 4, rows], held.at[s // 4, rows], new_out.at[s // 4, rows]))
    into = [pltpu.make_async_copy(a, b, sems.at[0, s]) for s, (a, b, _) in enumerate(ways)]
    out = [pltpu.make_async_copy(b, c, sems.at[1, s]) for s, (_, b, c) in enumerate(ways)]
    for copy in into:
        copy.start()
    for copy, then in zip(into, out):
        copy.wait()
        then.start()
    for copy in out:
        copy.wait()


def solution(mesh):
    return jax.shard_map(
        shards,
        mesh=mesh,
        in_specs=(P("dp", "mp"), P("dp", "mp", None), P("mp", None)),
        out_specs=(P("dp", "mp"), P("dp", "mp", None)),
        check_vma=False,
    )
```

```python
import jax
import jax.numpy as jnp
from jax import lax
from jax.experimental import pallas as pl
from jax.experimental.pallas import tpu as pltpu
from jax.sharding import PartitionSpec as P

ITERS = 6
BETA = 0.9
EPS = 1e-06
MESH = pl.DeviceIdType.MESH
BF = jnp.bfloat16
F32 = jnp.float32

WIDTH = 512
TILE = 128
COUNT = 16
ROWS = 8
PAIRS = [(i, j) for i in range(4) for j in range(i + 1, 4)]
SIZES = (5, 4)
PARTS = len(SIZES)
SPOT = [(p, n) for p, size in enumerate(SIZES) for n in range(size)]
BACK_SIZES = (5, 4)
BACKS = len(BACK_SIZES)
BACK_SPOT = [(p, n) for p, size in enumerate(BACK_SIZES) for n in range(size)]


def block(ref, i, j):
    return ref[i * TILE:(i + 1) * TILE, j * TILE:(j + 1) * TILE]


def packed(ref):
    half = TILE // 2
    diag = [block(ref, d, d) for d in range(4)]
    upper = [jnp.concatenate([diag[d][:half], diag[d + 1][:half]], axis=0) for d in (0, 2)]
    left = lax.broadcasted_iota(jnp.int32, (half, TILE), 1) < half
    lower = [jnp.where(left, pltpu.roll(diag[d + 1][half:], half, 1), diag[d][half:]) for d in (0, 2)]
    blocks = upper + [jnp.concatenate(lower, axis=0)] + [block(ref, i, j) for i, j in PAIRS]
    return [b.astype(BF).reshape(ROWS, 16, TILE) for b in blocks]


def unpacked(get):
    half = TILE // 2
    low = lax.broadcasted_iota(jnp.int32, (TILE, TILE), 0) >= half
    left = lax.broadcasted_iota(jnp.int32, (TILE, TILE), 1) < half
    corners = get(2)
    for d in range(4):
        upper = get(d // 2)[d % 2 * half:(d % 2 + 1) * half]
        corner = corners[d // 2 * half:(d // 2 + 1) * half]
        if d % 2:
            corner = pltpu.roll(corner, half, 1)
        whole = jnp.concatenate([upper, corner], axis=0)
        yield d, d, jnp.where(low & left, whole.T, whole)
    for n, (i, j) in enumerate(PAIRS):
        yield i, j, get(3 + n)


def kernel(
    owners_hbm, grad, state_hbm, update, new_hbm,
    state, owners, positions, inverse,
    packs, spreads, crosses, relays, landeds, chosens, factors, stat_packs, stat_alls,
    stat_picks, stat_backs, gfull, stat,
    m_ref, x_ref, b_ref, p_ref, f_ref, xl_ref, roots, raw_ref, sums_a, sums_b,
    s1s, s1r, s2s, s2r, s3s, s3r, gs, gr, r1s, r1r, r2s, r2r, r3s, r3r, rts, rtr, pas, par, pbs, pbr, loc,
):
    me = lax.axis_index("dp")
    mp = lax.axis_index("mp")
    row, r = lax.div(me, 8), lax.rem(me, 8)
    x, c = lax.div(r, 2), lax.rem(r, 2)
    zlo, y = lax.div(mp, 4), lax.rem(mp, 4)
    quad = lax.rem(x, 2) * 2 + c

    def send(src, dst, ssem, rsem, dp, mp_to=None):
        copy = pltpu.make_async_remote_copy(
            src_ref=src, dst_ref=dst, send_sem=ssem, recv_sem=rsem,
            device_id=(dp, mp if mp_to is None else mp_to), device_id_type=MESH,
        )
        copy.start()
        return copy

    def sent(groups):
        for copies in groups:
            for copy in copies:
                copy.wait_send()

    def row_peer(t):
        return lax.rem(r + t, 8)

    def plane_peer(dx, dy):
        to_x, to_y = lax.rem(x + dx, 4), lax.rem(y + dy, 4)
        return row * 8 + to_x * 2 + c, zlo * 4 + to_y

    def column_peer(dh, dl, dc):
        to_row, to_lo, to_c = lax.rem(row + dh, 4), lax.rem(zlo + dl, 2), lax.rem(c + dc, 2)
        return to_row * 8 + x * 2 + to_c, to_lo * 4 + y

    plane = [(dx, dy) for dx in range(4) for dy in range(4) if dx or dy]
    column = [(dh, dl, dc) for dh in range(4) for dl in range(2) for dc in range(2) if dh or dl or dc]

    loads = [pltpu.make_async_copy(state_hbm.at[k], state.at[k], loc.at[k]) for k in range(2)]
    for load in loads:
        load.start()
    own_grad = pltpu.make_async_copy(grad, gfull.at[quad], loc.at[2])
    own_grad.start()
    own_table = pltpu.make_async_copy(owners_hbm, owners, loc.at[3])
    own_table.start()
    barrier = pltpu.get_barrier_semaphore()
    greeted = [(row * 8 + row_peer(t), mp) for t in range(1, ROWS)]
    greeted += [plane_peer(dx, dy) for dx, dy in plane if dy]
    greeted += [column_peer(*d) for d in column if d[0] or d[1]]
    for peer in greeted:
        pl.semaphore_signal(barrier, inc=1, device_id=peer, device_id_type=MESH)

    for k in range(2):
        loads[k].wait()
        for (part, at), piece in zip(SPOT, packed(state.at[k])):
            packs[part][:, k, at] = piece
    for part in range(PARTS):
        spreads[part][pl.ds(2 * r, 2)] = packs[part][r]
    pl.semaphore_wait(barrier, len(greeted))

    stage1 = []
    for part in range(PARTS):
        copies = []
        for t in range(1, ROWS):
            peer = row_peer(t)
            s = part * 7 + t - 1
            copies.append(send(packs[part].at[peer], spreads[part].at[pl.ds(2 * r, 2)], s1s.at[s], s1r.at[s], row * 8 + peer))
        stage1.append(copies)
    own_grad.wait()
    other = x + 1 - 2 * lax.rem(x, 2)
    sibling = row * 8 + x * 2 + 1 - c
    own_rows = gfull.at[quad]
    g_copies = [
        send(own_rows, own_rows, gs.at[0], gr.at[0], row * 8 + other * 2 + c),
        send(own_rows, own_rows, gs.at[1], gr.at[1], sibling),
    ]

    own_table.wait()
    table = [owners[0, f] for f in range(COUNT)]
    place = []
    for f in range(COUNT):
        slot = jnp.int32(0)
        for g in range(f):
            slot = slot + jnp.where(table[g] == table[f], 1, 0)
        place.append(table[f] * 2 + slot)
        positions[f] = place[f]

    def invert(index, carry):
        target = row * 16 + index
        found = jnp.int32(-1)
        for f in range(COUNT):
            found = jnp.where(positions[f] == target, f, found)
        inverse[index] = found
        return carry

    lax.fori_loop(0, COUNT, invert, 0)

    wide = gfull[quad].astype(F32)
    grad_sum = jnp.sum(wide * wide, axis=0, keepdims=True)
    grad_sum = grad_sum[:, :128] + grad_sum[:, 128:256] + grad_sum[:, 256:384] + grad_sum[:, 384:]

    def turned(by):
        return lax.rem(row + by, 4)

    ways = (1, 3) * (PARTS // 2)
    back_ways = (1, 3)
    stage2 = []

    def cross(part):
        way = ways[part]
        for copy in stage1[part]:
            copy.wait_recv()

        def own(to_row, q):
            return spreads[part][jnp.clip(positions[to_row * 4 + q] - row * 16, 0, 15)]

        s = part * 3
        copies = []
        for q in range(4):
            crosses[part][0, q] = own(turned(2), q)
        copies.append(send(crosses[part].at[0], relays[part], s2s.at[s], s2r.at[s], turned(way) * 8 + r))
        for q in range(4):
            crosses[part][1, q] = own(turned(4 - way), q)
        copies.append(send(crosses[part].at[1], landeds[part].at[pl.ds(8, 4)], s2s.at[s + 1], s2r.at[s + 1], turned(4 - way) * 8 + r))
        for q in range(4):
            landeds[part][q] = own(row, q)
        stage2.append(copies)

    def merge(part):
        way = ways[part]
        stage2[part][0].wait_recv()
        s = part * 3
        for q in range(4):
            place_q = positions[turned(way) * 4 + q] - row * 16
            is_own = (place_q >= 0) & (place_q < 16)
            crosses[part][2, q] = jnp.where(is_own, spreads[part][jnp.clip(place_q, 0, 15)], relays[part][q])
        stage2[part].append(send(crosses[part].at[2], landeds[part].at[pl.ds(4, 4)], s2s.at[s + 2], s2r.at[s + 2], turned(way) * 8 + r))

    cross(0)
    cross(1)
    merge(0)
    g_copies[0].wait_recv()
    other_rows = gfull.at[lax.rem(other, 2) * 2 + c]
    g_copies.append(send(other_rows, other_rows, gs.at[2], gr.at[2], sibling))
    merge(1)

    g_copies[1].wait_recv()
    g_copies[2].wait_recv()
    g = gfull[...].reshape(WIDTH, WIDTH)

    @pl.when(c == 0)
    def _():
        stat[...] = lax.dot_general(g, g, (((1,), (1,)), ((), ())), preferred_element_type=F32)

    @pl.when(c == 1)
    def _():
        stat[...] = lax.dot_general(g.T, g, (((1,), (0,)), ((), ())), preferred_element_type=F32)

    mine = row * 4 + lax.div(x, 2) * 2 + c
    outer = lax.rem(x + 3 + 2 * lax.rem(x, 2), 4)
    back1 = []
    for (part, at), piece in zip(BACK_SPOT, packed(stat)):
        stat_packs[part][:, at] = piece
    for part in range(BACKS):
        stat_alls[part][mine] = stat_packs[part][r]
        copies = []
        for s, (to_x, to_c) in enumerate([(x, 1 - c), (outer, c), (outer, 1 - c)]):
            to, s = to_x * 2 + to_c, s + part * 3
            copies.append(send(stat_packs[part].at[to], stat_alls[part].at[mine], r1s.at[s], r1r.at[s], row * 8 + to))
        back1.append(copies)

    stage3 = []
    back2 = []
    for part in range(PARTS):
        stage2[part][1].wait_recv()
        stage2[part][2].wait_recv()
        for q in range(4):
            origin = lax.div(positions[row * 4 + q], 16)
            t = lax.rem(row - origin + 4, 4) if ways[part] == 1 else lax.rem(origin - row + 4, 4)
            chosens[part][q] = landeds[part][jnp.where(t >= 2, t - 1, t) * 4 + q]
        copies = []
        for t in range(1, ROWS):
            peer = row_peer(t)
            q = lax.div(peer, 4) * 2 + lax.rem(peer, 2)
            s = part * 7 + t - 1
            copies.append(send(chosens[part].at[q], factors[part].at[r], s3s.at[s], s3r.at[s], row * 8 + peer))
        factors[part][r] = chosens[part][lax.div(x, 2) * 2 + c]
        stage3.append(copies)

        if part == 0:
            for back, way in enumerate(back_ways):
                for copy in back1[back]:
                    copy.wait_recv()
                here = stat_alls[back].at[pl.ds(4 * row, 4)]
                s = back * 3
                copies = []
                for t, by in enumerate((way, 4 - way)):
                    copies.append(send(here, here, r2s.at[s + t], r2r.at[s + t], turned(by) * 8 + r))
                back2.append(copies)

    sent(stage1 + stage2 + back1 + [g_copies])

    norm = jnp.zeros((TILE, TILE), F32)
    def arrived(n):
        part, at = SPOT[n]
        if part not in here:
            here.append(part)
            for copy in stage3[part]:
                copy.wait_recv()
        return factors[part][:, at].reshape(TILE, TILE).astype(F32)

    here = []
    for i, j, old in unpacked(arrived):
        mixed = BETA * old + (1.0 - BETA) * block(stat, i, j)
        m_ref[i * TILE:(i + 1) * TILE, j * TILE:(j + 1) * TILE] = mixed
        if i == j:
            norm = norm + mixed * mixed
        else:
            m_ref[j * TILE:(j + 1) * TILE, i * TILE:(i + 1) * TILE] = mixed.T
            norm = norm + 2.0 * (mixed * mixed)
    total = jnp.sum(jnp.sum(norm, axis=0, keepdims=True), axis=1, keepdims=True)
    scale = jnp.sqrt(total + EPS)
    inverse_scale = 1.0 / scale
    start = lax.rsqrt(jnp.sqrt(scale))

    further = []
    for part, way in enumerate(back_ways):
        here = stat_alls[part].at[pl.ds(4 * turned(4 - way), 4)]
        s = part * 3 + 2
        further.append(pltpu.make_async_remote_copy(
            src_ref=here, dst_ref=here, send_sem=r2s.at[s], recv_sem=r2r.at[s],
            device_id=(turned(way) * 8 + r, mp), device_id_type=MESH,
        ))

    HALF = WIDTH // 2
    halves = [pl.ds(h * HALF, HALF) for h in range(2)]
    for h, rows in enumerate(halves):
        reduced = m_ref[rows] * inverse_scale
        m_ref[rows] = reduced
        b_ref[rows] = reduced.astype(BF)
        at = lax.broadcasted_iota(jnp.int32, (HALF, WIDTH), 0) + h * HALF
        eye = at == lax.broadcasted_iota(jnp.int32, (HALF, WIDTH), 1)
        x_ref[rows] = jnp.where(eye, start, 0.0)

    def dot(a, b):
        return jnp.dot(a, b, preferred_element_type=F32)

    def apply(cols):
        return 1.25 * x_ref[:, cols] - 0.25 * dot(xl_ref[...], b_ref[:, cols])

    def step(index, carry):
        @pl.when(index == 2)
        def _():
            for part in range(BACKS):
                back2[part][0].wait_recv()
                further[part].start()

        xl_ref[...] = x_ref[...].astype(BF)
        for cols in halves:
            p_ref[:, cols] = (dot(b_ref[...], b_ref[:, cols]) * 0.0625 - 0.625 * b_ref[:, cols].astype(F32)).astype(BF)
        x_ref[:, halves[0]] = apply(halves[0])
        for cols in halves:
            f_ref[:, cols] = (dot(p_ref[...], p_ref[:, cols]) + 3.125 * p_ref[:, cols].astype(F32)).astype(BF)
        x_ref[:, halves[1]] = apply(halves[1])
        for cols in halves:
            after = 2.44140625 * m_ref[:, cols] + dot(f_ref[...], b_ref[:, cols])
            m_ref[:, cols] = after
            b_ref[:, cols] = after.astype(BF)
        return carry

    lax.fori_loop(0, ITERS - 1, step, 0)
    for part in range(BACKS):
        back2[part].append(further[part])

    root_copies = []
    xl_ref[...] = x_ref[...].astype(BF)
    for h, cols in enumerate(halves):
        roots[c, :, cols] = apply(cols).astype(BF)
        here = roots.at[c, :, cols]
        root_copies.append(send(here, here, rts.at[h], rtr.at[h], sibling))

    for copies in back2:
        copies[1].wait_recv()
        copies[2].wait_recv()
    back3 = []
    for part in range(BACKS):
        for t in range(1, ROWS):
            peer = row_peer(t)
            for k in range(2):
                stat_picks[part][t - 1, k] = stat_alls[part][jnp.maximum(inverse[2 * peer + k], 0)]
            s = part * 7 + t - 1
            back3.append(send(stat_picks[part].at[t - 1], stat_backs[part].at[r], r3s.at[s], r3r.at[s], row * 8 + peer))
        for k in range(2):
            stat_backs[part][r, k] = stat_alls[part][jnp.maximum(inverse[2 * r + k], 0)]

    for copy in root_copies:
        copy.wait_recv()
    left = roots[0, pl.ds(quad * TILE, TILE)]
    first = dot(left, gfull[...].reshape(WIDTH, WIDTH)).astype(BF)
    raw = dot(first, roots[1])
    raw_ref[...] = raw
    raw_sum = jnp.sum(raw * raw, axis=0, keepdims=True)
    raw_sum = raw_sum[:, :128] + raw_sum[:, 128:256] + raw_sum[:, 256:384] + raw_sum[:, 384:]

    v = row * 4 + zlo * 2 + c
    sums_a[v, :, :128] = grad_sum
    sums_a[v, :, 128:] = raw_sum
    round_a = []
    for s, d in enumerate(column):
        dp, to_mp = column_peer(*d)
        round_a.append(send(sums_a.at[v], sums_a.at[v], pas.at[s], par.at[s], dp, to_mp))
    sent(stage3 + back2 + [root_copies])
    for copy in round_a:
        copy.wait_recv()
    u = x * 4 + y
    sums_b[u] = jnp.sum(sums_a[...], axis=0)
    round_b = []
    for s, d in enumerate(plane):
        dp, to_mp = plane_peer(*d)
        round_b.append(send(sums_b.at[u], sums_b.at[u], pbs.at[s], pbr.at[s], dp, to_mp))

    sent([round_a, back3, round_b])

    for copy in back3:
        copy.wait_recv()
    stores = []
    for k in range(2):
        present = inverse[2 * r + k] >= 0

        def returned(n):
            part, at = BACK_SPOT[n]
            return stat_backs[part][:, k, at].reshape(TILE, TILE).astype(F32)

        for i, j, got in unpacked(returned):
            for a, b, value in ((i, j, got),) + (((j, i, got.T),) if i != j else ()):
                old = state[k, a * TILE:(a + 1) * TILE, b * TILE:(b + 1) * TILE]
                state[k, a * TILE:(a + 1) * TILE, b * TILE:(b + 1) * TILE] = jnp.where(
                    present, BETA * old + (1.0 - BETA) * value, old
                )
        store = pltpu.make_async_copy(state.at[k], new_hbm.at[k], loc.at[k])
        store.start()
        stores.append(store)

    for copy in round_b:
        copy.wait_recv()
    both = jnp.sum(sums_b[...], axis=0)
    grad_total = jnp.sum(both[:, :128], axis=1, keepdims=True)
    raw_total = jnp.sum(both[:, 128:], axis=1, keepdims=True)
    ratio = jnp.sqrt(grad_total / (raw_total + EPS))
    update[...] = (raw_ref[...] * ratio).astype(BF)

    for store in stores:
        store.wait()


def shards(grad, stat_state, owners):
    dma = pltpu.SemaphoreType.DMA
    vm = pltpu.VMEM

    def parted(*shape):
        return [vm(shape + (size, 16, TILE), BF) for size in SIZES]

    def backed(*shape):
        return [vm(shape + (size, 16, TILE), BF) for size in BACK_SIZES]

    sems = []
    for count in (7 * PARTS, 3 * PARTS, 7 * PARTS, 3, 3 * BACKS, 3 * BACKS, 7 * BACKS, 2, 15, 15):
        sems += [dma((count,)), dma((count,))]
    square = (WIDTH, WIDTH)
    results = pl.pallas_call(
        kernel,
        out_shape=(
            jax.ShapeDtypeStruct((TILE, WIDTH), BF),
            jax.ShapeDtypeStruct((2, WIDTH, WIDTH), F32),
        ),
        in_specs=[
            pl.BlockSpec(memory_space=pltpu.HBM),
            pl.BlockSpec(memory_space=pltpu.HBM),
            pl.BlockSpec(memory_space=pltpu.HBM),
        ],
        out_specs=(pl.BlockSpec(memory_space=pltpu.VMEM), pl.BlockSpec(memory_space=pl.ANY)),
        scratch_shapes=[
            vm((2, WIDTH, WIDTH), F32),
            pltpu.SMEM((1, COUNT), jnp.int32),
            pltpu.SMEM((COUNT,), jnp.int32),
            pltpu.SMEM((COUNT,), jnp.int32),
            parted(ROWS, 2), parted(16), parted(3, 4), parted(4), parted(12), parted(4), parted(ROWS),
            backed(ROWS), backed(COUNT), backed(7, 2), backed(ROWS, 2),
            vm((4, TILE, WIDTH), BF),
            vm(square, F32),
            vm(square, F32), vm(square, F32), vm(square, BF), vm(square, BF), vm(square, BF), vm(square, BF),
            vm((2, WIDTH, WIDTH), BF),
            vm((TILE, WIDTH), F32),
            vm((16, 1, 256), F32),
            vm((16, 1, 256), F32),
            *sems,
            dma((4,)),
        ],
        compiler_params=pltpu.CompilerParams(
            collective_id=0, has_side_effects=True, vmem_limit_bytes=60 * 1024 * 1024
        ),
    )(owners, grad, stat_state)
    hbm = pl.BlockSpec(memory_space=pltpu.HBM)
    return pl.pallas_call(
        hand_over,
        out_shape=tuple(jax.ShapeDtypeStruct(a.shape, a.dtype) for a in results),
        in_specs=[hbm, hbm],
        out_specs=(hbm, hbm),
        scratch_shapes=[vm((2, WIDTH, WIDTH), F32), vm((TILE, WIDTH), BF), dma((2, 9))],
        compiler_params=pltpu.CompilerParams(vmem_limit_bytes=60 * 1024 * 1024),
    )(*results)


def hand_over(update, new, update_out, new_out, held, held_update, sems):
    ways = [(update, held_update, update_out)]
    for s in range(8):
        rows = pl.ds(s % 4 * TILE, TILE)
        ways.append((new.at[s // 4, rows], held.at[s // 4, rows], new_out.at[s // 4, rows]))
    into = [pltpu.make_async_copy(a, b, sems.at[0, s]) for s, (a, b, _) in enumerate(ways)]
    out = [pltpu.make_async_copy(b, c, sems.at[1, s]) for s, (_, b, c) in enumerate(ways)]
    for copy in into:
        copy.start()
    for copy, then in zip(into, out):
        copy.wait()
        then.start()
    for copy in out:
        copy.wait()


def solution(mesh):
    return jax.shard_map(
        shards,
        mesh=mesh,
        in_specs=(P("dp", "mp"), P("dp", "mp", None), P("mp", None)),
        out_specs=(P("dp", "mp"), P("dp", "mp", None)),
        check_vma=False,
    )
```

```python
import jax
import jax.numpy as jnp
from jax import lax
from jax.experimental import pallas as pl
from jax.experimental.pallas import tpu as pltpu
from jax.sharding import PartitionSpec as P

ITERS = 6
BETA = 0.9
EPS = 1e-06
MESH = pl.DeviceIdType.MESH
BF = jnp.bfloat16
F32 = jnp.float32

WIDTH = 512
TILE = 128
COUNT = 16
ROWS = 8
PAIRS = [(i, j) for i in range(4) for j in range(i + 1, 4)]
SIZES = (5, 4)
PARTS = len(SIZES)
SPOT = [(p, n) for p, size in enumerate(SIZES) for n in range(size)]
BACK_SIZES = (5, 4)
BACKS = len(BACK_SIZES)
BACK_SPOT = [(p, n) for p, size in enumerate(BACK_SIZES) for n in range(size)]


def block(ref, i, j):
    return ref[i * TILE:(i + 1) * TILE, j * TILE:(j + 1) * TILE]


def packed(ref):
    half = TILE // 2
    diag = [block(ref, d, d) for d in range(4)]
    upper = [jnp.concatenate([diag[d][:half], diag[d + 1][:half]], axis=0) for d in (0, 2)]
    left = lax.broadcasted_iota(jnp.int32, (half, TILE), 1) < half
    lower = [jnp.where(left, pltpu.roll(diag[d + 1][half:], half, 1), diag[d][half:]) for d in (0, 2)]
    blocks = upper + [jnp.concatenate(lower, axis=0)] + [block(ref, i, j) for i, j in PAIRS]
    return [b.astype(BF).reshape(ROWS, 16, TILE) for b in blocks]


def unpacked(get):
    half = TILE // 2
    low = lax.broadcasted_iota(jnp.int32, (TILE, TILE), 0) >= half
    left = lax.broadcasted_iota(jnp.int32, (TILE, TILE), 1) < half
    corners = get(2)
    for d in range(4):
        upper = get(d // 2)[d % 2 * half:(d % 2 + 1) * half]
        corner = corners[d // 2 * half:(d // 2 + 1) * half]
        if d % 2:
            corner = pltpu.roll(corner, half, 1)
        whole = jnp.concatenate([upper, corner], axis=0)
        yield d, d, jnp.where(low & left, whole.T, whole)
    for n, (i, j) in enumerate(PAIRS):
        yield i, j, get(3 + n)


def kernel(
    owners_hbm, grad, state_hbm, update, new_hbm,
    state, owners, positions, inverse,
    packs, spreads, crosses, relays, landeds, chosens, factors, stat_packs, stat_alls,
    stat_picks, stat_backs, gfull, stat,
    m_ref, x_ref, b_ref, p_ref, f_ref, xl_ref, roots, raw_ref, sums_a, sums_b,
    s1s, s1r, s2s, s2r, s3s, s3r, gs, gr, r1s, r1r, r2s, r2r, r3s, r3r, rts, rtr, pas, par, pbs, pbr, loc,
):
    me = lax.axis_index("dp")
    mp = lax.axis_index("mp")
    row, r = lax.div(me, 8), lax.rem(me, 8)
    x, c = lax.div(r, 2), lax.rem(r, 2)
    zlo, y = lax.div(mp, 4), lax.rem(mp, 4)
    quad = lax.rem(x, 2) * 2 + c

    def send(src, dst, ssem, rsem, dp, mp_to=None):
        copy = pltpu.make_async_remote_copy(
            src_ref=src, dst_ref=dst, send_sem=ssem, recv_sem=rsem,
            device_id=(dp, mp if mp_to is None else mp_to), device_id_type=MESH,
        )
        copy.start()
        return copy

    def sent(groups):
        for copies in groups:
            for copy in copies:
                copy.wait_send()

    def row_peer(t):
        return lax.rem(r + t, 8)

    def plane_peer(dx, dy):
        to_x, to_y = lax.rem(x + dx, 4), lax.rem(y + dy, 4)
        return row * 8 + to_x * 2 + c, zlo * 4 + to_y

    def column_peer(dh, dl, dc):
        to_row, to_lo, to_c = lax.rem(row + dh, 4), lax.rem(zlo + dl, 2), lax.rem(c + dc, 2)
        return to_row * 8 + x * 2 + to_c, to_lo * 4 + y

    plane = [(dx, dy) for dx in range(4) for dy in range(4) if dx or dy]
    column = [(dh, dl, dc) for dh in range(4) for dl in range(2) for dc in range(2) if dh or dl or dc]

    loads = [pltpu.make_async_copy(state_hbm.at[k], state.at[k], loc.at[k]) for k in range(2)]
    for load in loads:
        load.start()
    own_grad = pltpu.make_async_copy(grad, gfull.at[quad], loc.at[2])
    own_grad.start()
    own_table = pltpu.make_async_copy(owners_hbm, owners, loc.at[3])
    own_table.start()
    barrier = pltpu.get_barrier_semaphore()
    greeted = [(row * 8 + row_peer(t), mp) for t in range(1, ROWS)]
    greeted += [plane_peer(dx, dy) for dx, dy in plane if dy]
    greeted += [column_peer(*d) for d in column if d[0] or d[1]]
    for peer in greeted:
        pl.semaphore_signal(barrier, inc=1, device_id=peer, device_id_type=MESH)

    for k in range(2):
        loads[k].wait()
        for (part, at), piece in zip(SPOT, packed(state.at[k])):
            packs[part][:, k, at] = piece
    for part in range(PARTS):
        spreads[part][pl.ds(2 * r, 2)] = packs[part][r]
    pl.semaphore_wait(barrier, len(greeted))

    stage1 = []
    for part in range(PARTS):
        copies = []
        for t in range(1, ROWS):
            peer = row_peer(t)
            s = part * 7 + t - 1
            copies.append(send(packs[part].at[peer], spreads[part].at[pl.ds(2 * r, 2)], s1s.at[s], s1r.at[s], row * 8 + peer))
        stage1.append(copies)
    own_grad.wait()
    other = x + 1 - 2 * lax.rem(x, 2)
    sibling = row * 8 + x * 2 + 1 - c
    own_rows = gfull.at[quad]
    g_copies = [
        send(own_rows, own_rows, gs.at[0], gr.at[0], row * 8 + other * 2 + c),
        send(own_rows, own_rows, gs.at[1], gr.at[1], sibling),
    ]

    own_table.wait()
    table = [owners[0, f] for f in range(COUNT)]
    place = []
    for f in range(COUNT):
        slot = jnp.int32(0)
        for g in range(f):
            slot = slot + jnp.where(table[g] == table[f], 1, 0)
        place.append(table[f] * 2 + slot)
        positions[f] = place[f]

    def invert(index, carry):
        target = row * 16 + index
        found = jnp.int32(-1)
        for f in range(COUNT):
            found = jnp.where(positions[f] == target, f, found)
        inverse[index] = found
        return carry

    lax.fori_loop(0, COUNT, invert, 0)

    wide = gfull[quad].astype(F32)
    grad_sum = jnp.sum(wide * wide, axis=0, keepdims=True)
    grad_sum = grad_sum[:, :128] + grad_sum[:, 128:256] + grad_sum[:, 256:384] + grad_sum[:, 384:]

    def turned(by):
        return lax.rem(row + by, 4)

    ways = (1, 3) * (PARTS // 2)
    back_ways = (1, 3)
    stage2 = []

    def cross(part):
        way = ways[part]
        for copy in stage1[part]:
            copy.wait_recv()

        def own(to_row, q):
            return spreads[part][jnp.clip(positions[to_row * 4 + q] - row * 16, 0, 15)]

        s = part * 3
        copies = []
        for q in range(4):
            crosses[part][0, q] = own(turned(2), q)
        copies.append(send(crosses[part].at[0], relays[part], s2s.at[s], s2r.at[s], turned(way) * 8 + r))
        for q in range(4):
            crosses[part][1, q] = own(turned(4 - way), q)
        copies.append(send(crosses[part].at[1], landeds[part].at[pl.ds(8, 4)], s2s.at[s + 1], s2r.at[s + 1], turned(4 - way) * 8 + r))
        for q in range(4):
            landeds[part][q] = own(row, q)
        stage2.append(copies)

    def merge(part):
        way = ways[part]
        stage2[part][0].wait_recv()
        s = part * 3
        for q in range(4):
            place_q = positions[turned(way) * 4 + q] - row * 16
            is_own = (place_q >= 0) & (place_q < 16)
            crosses[part][2, q] = jnp.where(is_own, spreads[part][jnp.clip(place_q, 0, 15)], relays[part][q])
        stage2[part].append(send(crosses[part].at[2], landeds[part].at[pl.ds(4, 4)], s2s.at[s + 2], s2r.at[s + 2], turned(way) * 8 + r))

    cross(0)
    cross(1)
    merge(0)
    g_copies[0].wait_recv()
    other_rows = gfull.at[lax.rem(other, 2) * 2 + c]
    g_copies.append(send(other_rows, other_rows, gs.at[2], gr.at[2], sibling))
    merge(1)

    g_copies[1].wait_recv()
    g_copies[2].wait_recv()
    g = gfull[...].reshape(WIDTH, WIDTH)

    @pl.when(c == 0)
    def _():
        stat[...] = lax.dot_general(g, g, (((1,), (1,)), ((), ())), preferred_element_type=F32)

    @pl.when(c == 1)
    def _():
        stat[...] = lax.dot_general(g.T, g, (((1,), (0,)), ((), ())), preferred_element_type=F32)

    mine = row * 4 + lax.div(x, 2) * 2 + c
    outer = lax.rem(x + 3 + 2 * lax.rem(x, 2), 4)
    back1 = []
    for (part, at), piece in zip(BACK_SPOT, packed(stat)):
        stat_packs[part][:, at] = piece
    for part in range(BACKS):
        stat_alls[part][mine] = stat_packs[part][r]
        copies = []
        for s, (to_x, to_c) in enumerate([(x, 1 - c), (outer, c), (outer, 1 - c)]):
            to, s = to_x * 2 + to_c, s + part * 3
            copies.append(send(stat_packs[part].at[to], stat_alls[part].at[mine], r1s.at[s], r1r.at[s], row * 8 + to))
        back1.append(copies)

    stage3 = []
    back2 = []
    for part in range(PARTS):
        stage2[part][1].wait_recv()
        stage2[part][2].wait_recv()
        for q in range(4):
            origin = lax.div(positions[row * 4 + q], 16)
            t = lax.rem(row - origin + 4, 4) if ways[part] == 1 else lax.rem(origin - row + 4, 4)
            chosens[part][q] = landeds[part][jnp.where(t >= 2, t - 1, t) * 4 + q]
        copies = []
        for t in range(1, ROWS):
            peer = row_peer(t)
            q = lax.div(peer, 4) * 2 + lax.rem(peer, 2)
            s = part * 7 + t - 1
            copies.append(send(chosens[part].at[q], factors[part].at[r], s3s.at[s], s3r.at[s], row * 8 + peer))
        factors[part][r] = chosens[part][lax.div(x, 2) * 2 + c]
        stage3.append(copies)

        if part == 0:
            for back, way in enumerate(back_ways):
                for copy in back1[back]:
                    copy.wait_recv()
                here = stat_alls[back].at[pl.ds(4 * row, 4)]
                s = back * 3
                copies = []
                for t, by in enumerate((way, 4 - way)):
                    copies.append(send(here, here, r2s.at[s + t], r2r.at[s + t], turned(by) * 8 + r))
                back2.append(copies)

    sent(stage1 + stage2 + back1 + [g_copies])

    norm = jnp.zeros((TILE, TILE), F32)
    def arrived(n):
        part, at = SPOT[n]
        if part not in here:
            here.append(part)
            for copy in stage3[part]:
                copy.wait_recv()
        return factors[part][:, at].reshape(TILE, TILE).astype(F32)

    here = []
    for i, j, old in unpacked(arrived):
        mixed = BETA * old + (1.0 - BETA) * block(stat, i, j)
        m_ref[i * TILE:(i + 1) * TILE, j * TILE:(j + 1) * TILE] = mixed
        if i == j:
            norm = norm + mixed * mixed
        else:
            m_ref[j * TILE:(j + 1) * TILE, i * TILE:(i + 1) * TILE] = mixed.T
            norm = norm + 2.0 * (mixed * mixed)
    total = jnp.sum(jnp.sum(norm, axis=0, keepdims=True), axis=1, keepdims=True)
    scale = jnp.sqrt(total + EPS)
    inverse_scale = 1.0 / scale
    start = lax.rsqrt(jnp.sqrt(scale))

    further = []
    for part, way in enumerate(back_ways):
        here = stat_alls[part].at[pl.ds(4 * turned(4 - way), 4)]
        s = part * 3 + 2
        further.append(pltpu.make_async_remote_copy(
            src_ref=here, dst_ref=here, send_sem=r2s.at[s], recv_sem=r2r.at[s],
            device_id=(turned(way) * 8 + r, mp), device_id_type=MESH,
        ))

    HALF = WIDTH // 2
    halves = [pl.ds(h * HALF, HALF) for h in range(2)]
    for h, rows in enumerate(halves):
        reduced = m_ref[rows] * inverse_scale
        m_ref[rows] = reduced
        b_ref[rows] = reduced.astype(BF)
        at = lax.broadcasted_iota(jnp.int32, (HALF, WIDTH), 0) + h * HALF
        eye = at == lax.broadcasted_iota(jnp.int32, (HALF, WIDTH), 1)
        x_ref[rows] = jnp.where(eye, start, 0.0)

    def dot(a, b):
        return jnp.dot(a, b, preferred_element_type=F32)

    def apply(cols):
        return 1.25 * x_ref[:, cols] - 0.25 * dot(xl_ref[...], b_ref[:, cols])

    def step(index, carry):
        @pl.when(index == 1)
        def _():
            for part in range(BACKS):
                back2[part][0].wait_recv()
                further[part].start()

        xl_ref[...] = x_ref[...].astype(BF)
        for cols in halves:
            p_ref[:, cols] = (dot(b_ref[...], b_ref[:, cols]) * 0.0625 - 0.625 * b_ref[:, cols].astype(F32)).astype(BF)
        x_ref[:, halves[0]] = apply(halves[0])
        for cols in halves:
            f_ref[:, cols] = (dot(p_ref[...], p_ref[:, cols]) + 3.125 * p_ref[:, cols].astype(F32)).astype(BF)
        x_ref[:, halves[1]] = apply(halves[1])
        for cols in halves:
            after = 2.44140625 * m_ref[:, cols] + dot(f_ref[...], b_ref[:, cols])
            m_ref[:, cols] = after
            b_ref[:, cols] = after.astype(BF)
        return carry

    lax.fori_loop(0, ITERS - 1, step, 0)
    for part in range(BACKS):
        back2[part].append(further[part])

    root_copies = []
    xl_ref[...] = x_ref[...].astype(BF)
    for h, cols in enumerate(halves):
        roots[c, :, cols] = apply(cols).astype(BF)
        here = roots.at[c, :, cols]
        root_copies.append(send(here, here, rts.at[h], rtr.at[h], sibling))

    for copies in back2:
        copies[1].wait_recv()
        copies[2].wait_recv()
    back3 = []
    for part in range(BACKS):
        for t in range(1, ROWS):
            peer = row_peer(t)
            for k in range(2):
                stat_picks[part][t - 1, k] = stat_alls[part][jnp.maximum(inverse[2 * peer + k], 0)]
            s = part * 7 + t - 1
            back3.append(send(stat_picks[part].at[t - 1], stat_backs[part].at[r], r3s.at[s], r3r.at[s], row * 8 + peer))
        for k in range(2):
            stat_backs[part][r, k] = stat_alls[part][jnp.maximum(inverse[2 * r + k], 0)]

    for copy in root_copies:
        copy.wait_recv()
    left = roots[0, pl.ds(quad * TILE, TILE)]
    first = dot(left, gfull[...].reshape(WIDTH, WIDTH)).astype(BF)
    raw = dot(first, roots[1])
    raw_ref[...] = raw
    raw_sum = jnp.sum(raw * raw, axis=0, keepdims=True)
    raw_sum = raw_sum[:, :128] + raw_sum[:, 128:256] + raw_sum[:, 256:384] + raw_sum[:, 384:]

    v = row * 4 + zlo * 2 + c
    sums_a[v, :, :128] = grad_sum
    sums_a[v, :, 128:] = raw_sum
    round_a = []
    for s, d in enumerate(column):
        dp, to_mp = column_peer(*d)
        round_a.append(send(sums_a.at[v], sums_a.at[v], pas.at[s], par.at[s], dp, to_mp))
    sent(stage3 + back2 + [root_copies])
    for copy in round_a:
        copy.wait_recv()
    u = x * 4 + y
    sums_b[u] = jnp.sum(sums_a[...], axis=0)
    round_b = []
    for s, d in enumerate(plane):
        dp, to_mp = plane_peer(*d)
        round_b.append(send(sums_b.at[u], sums_b.at[u], pbs.at[s], pbr.at[s], dp, to_mp))


    for copy in back3:
        copy.wait_recv()
    stores = []
    for k in range(2):
        present = inverse[2 * r + k] >= 0

        def returned(n):
            part, at = BACK_SPOT[n]
            return stat_backs[part][:, k, at].reshape(TILE, TILE).astype(F32)

        for i, j, got in unpacked(returned):
            for a, b, value in ((i, j, got),) + (((j, i, got.T),) if i != j else ()):
                old = state[k, a * TILE:(a + 1) * TILE, b * TILE:(b + 1) * TILE]
                state[k, a * TILE:(a + 1) * TILE, b * TILE:(b + 1) * TILE] = jnp.where(
                    present, BETA * old + (1.0 - BETA) * value, old
                )
        store = pltpu.make_async_copy(state.at[k], new_hbm.at[k], loc.at[k])
        store.start()
        stores.append(store)

    sent([round_a, back3, round_b])
    for copy in round_b:
        copy.wait_recv()
    both = jnp.sum(sums_b[...], axis=0)
    grad_total = jnp.sum(both[:, :128], axis=1, keepdims=True)
    raw_total = jnp.sum(both[:, 128:], axis=1, keepdims=True)
    ratio = jnp.sqrt(grad_total / (raw_total + EPS))
    update[...] = (raw_ref[...] * ratio).astype(BF)

    for store in stores:
        store.wait()


def shards(grad, stat_state, owners):
    dma = pltpu.SemaphoreType.DMA
    vm = pltpu.VMEM

    def parted(*shape):
        return [vm(shape + (size, 16, TILE), BF) for size in SIZES]

    def backed(*shape):
        return [vm(shape + (size, 16, TILE), BF) for size in BACK_SIZES]

    sems = []
    for count in (7 * PARTS, 3 * PARTS, 7 * PARTS, 3, 3 * BACKS, 3 * BACKS, 7 * BACKS, 2, 15, 15):
        sems += [dma((count,)), dma((count,))]
    square = (WIDTH, WIDTH)
    results = pl.pallas_call(
        kernel,
        out_shape=(
            jax.ShapeDtypeStruct((TILE, WIDTH), BF),
            jax.ShapeDtypeStruct((2, WIDTH, WIDTH), F32),
        ),
        in_specs=[
            pl.BlockSpec(memory_space=pltpu.HBM),
            pl.BlockSpec(memory_space=pltpu.HBM),
            pl.BlockSpec(memory_space=pltpu.HBM),
        ],
        out_specs=(pl.BlockSpec(memory_space=pltpu.VMEM), pl.BlockSpec(memory_space=pl.ANY)),
        scratch_shapes=[
            vm((2, WIDTH, WIDTH), F32),
            pltpu.SMEM((1, COUNT), jnp.int32),
            pltpu.SMEM((COUNT,), jnp.int32),
            pltpu.SMEM((COUNT,), jnp.int32),
            parted(ROWS, 2), parted(16), parted(3, 4), parted(4), parted(12), parted(4), parted(ROWS),
            backed(ROWS), backed(COUNT), backed(7, 2), backed(ROWS, 2),
            vm((4, TILE, WIDTH), BF),
            vm(square, F32),
            vm(square, F32), vm(square, F32), vm(square, BF), vm(square, BF), vm(square, BF), vm(square, BF),
            vm((2, WIDTH, WIDTH), BF),
            vm((TILE, WIDTH), F32),
            vm((16, 1, 256), F32),
            vm((16, 1, 256), F32),
            *sems,
            dma((4,)),
        ],
        compiler_params=pltpu.CompilerParams(
            collective_id=0, has_side_effects=True, vmem_limit_bytes=60 * 1024 * 1024
        ),
    )(owners, grad, stat_state)
    hbm = pl.BlockSpec(memory_space=pltpu.HBM)
    return pl.pallas_call(
        hand_over,
        out_shape=tuple(jax.ShapeDtypeStruct(a.shape, a.dtype) for a in results),
        in_specs=[hbm, hbm],
        out_specs=(hbm, hbm),
        scratch_shapes=[vm((2, WIDTH, WIDTH), F32), vm((TILE, WIDTH), BF), dma((2, 9))],
        compiler_params=pltpu.CompilerParams(vmem_limit_bytes=60 * 1024 * 1024),
    )(*results)


def hand_over(update, new, update_out, new_out, held, held_update, sems):
    ways = [(update, held_update, update_out)]
    for s in range(8):
        rows = pl.ds(s % 4 * TILE, TILE)
        ways.append((new.at[s // 4, rows], held.at[s // 4, rows], new_out.at[s // 4, rows]))
    into = [pltpu.make_async_copy(a, b, sems.at[0, s]) for s, (a, b, _) in enumerate(ways)]
    out = [pltpu.make_async_copy(b, c, sems.at[1, s]) for s, (_, b, c) in enumerate(ways)]
    for copy in into:
        copy.start()
    for copy, then in zip(into, out):
        copy.wait()
        then.start()
    for copy in out:
        copy.wait()


def solution(mesh):
    return jax.shard_map(
        shards,
        mesh=mesh,
        in_specs=(P("dp", "mp"), P("dp", "mp", None), P("mp", None)),
        out_specs=(P("dp", "mp"), P("dp", "mp", None)),
        check_vma=False,
    )
```
